32 devices in a mesh: expert: 4 (over x, core), shard: 8 (over z, y).
Axes of the slice: x: 2, y: 2, z: 4, core: 2. Of those that a mesh axis runs over, the one named last changes fastest.
Arguments:
- tokens: bfloat16 [8, 1024, 1536], P('shard', 'expert'), may hold values from -6 to 6
- segment_ids: int32 [8, 1024], P('shard', 'expert'), may hold values from 0 to 3, never falling along the last dimension, each value on 1 to 769 neighbouring positions
- routes: int32 [8, 1024, 8], P('shard', 'expert'), may hold values from 0 to 19, all different within a row; in each aligned block of 256 rows (0 to 255, 256 to 511, ..., all dimensions but the last counted through in order) at most 184 rows name the same one
- gain_attn: bfloat16 [1536], P('shard'), may hold values from 0.5 to 1.5
- w_query: bfloat16 [1536, 1536], P('shard'), may hold values from -0.15625 to 0.15625
- key_weight: bfloat16 [1536, 512], P('shard'), may hold values from -0.15625 to 0.15625
- value_weight: bfloat16 [1536, 512], P('shard'), may hold values from -0.15625 to 0.15625
- w_out: bfloat16 [1536, 1536], P('shard'), may hold values from -0.625 to 0.625
- gain_ffn: bfloat16 [1536], P('shard'), may hold values from 0.5 to 1.5
- w_router: bfloat16 [1536, 20], P('shard'), may hold values from -0.078125 to 0.078125
- w_gate_up: bfloat16 [1536, 20, 1024], P('shard', 'expert'), may hold values from -0.3125 to 0.3125
- w_down: bfloat16 [1536, 20, 512], P('shard', 'expert'), may hold values from -0.3125 to 0.3125
- cotangent: bfloat16 [8, 1024, 1536], P('shard', 'expert'), may hold values from -6 to 6
Outputs:
- mixed: bfloat16 [8, 1024, 1536], P('shard', 'expert')
- grad_tokens: bfloat16 [8, 1024, 1536], P('shard', 'expert')
- grad_gain_attn: float32 [1536], P(('expert', 'shard'))
- grad_query: float32 [1536, 1536], P(('expert', 'shard'))
- grad_key: float32 [1536, 512], P(('expert', 'shard'))
- grad_value: float32 [1536, 512], P(('expert', 'shard'))
- grad_out: float32 [1536, 1536], P(('expert', 'shard'))
- grad_gain_ffn: float32 [1536], P(('expert', 'shard'))
- grad_router: float32 [1536, 20], P(('expert', 'shard'))
- grad_gate_up: float32 [1536, 20, 1024], P('shard', 'expert')
- grad_down: float32 [1536, 20, 512], P('shard', 'expert')
The draws below stay inside these ranges and needn't reach their ends.
Inputs may be any that keep to these rules, and one draw needn't show every extreme that they name: `routes`: each token names 8 different experts. Among the 256 token rows of one device no expert is named more than 184 times, and in every draw some device's rows name some expert exactly 184 times. `segment_ids`: document numbers never fall along a sequence; every document has at most 769 positions, and one of each sequence has exactly that many.
All inputs are finite; a program needn't handle non-finite values.
Results may differ from the reference program's by a relative error of at most 0.019.
Values may be sent and summed in bfloat16 or wider, within the bound.
No kernel may reach another device: no remote copies, remote signals or barrier semaphores. Data moves between devices by JAX's collectives and lax.ppermute only.
A program may use at most 448 MiB of HBM per device.

```python
import math
import jax
import jax.numpy as jnp
import numpy as np
from jax import lax

MODEL_DIM = 1536
QUERY_HEADS = 24
KEY_VALUE_HEADS = 8
HEAD_SIZE = 64
FF = 512
TOP = 8
SEGS = 4
TOK_DEV = 256
EXPERTS = 20
SEQ = 1024
GROUPS = 8
CAP = 184


def block_scale(stream_key, shape, split, smallest, largest):
    gain = 1.0
    for position, blocks in split:
        draws = jax.random.uniform(jax.random.fold_in(jax.random.fold_in(stream_key, 6), position), (blocks,), jnp.float32, smallest / len(split), largest / len(split))
        gain = gain * jnp.repeat(jnp.exp(draws), shape[position] // blocks).reshape((-1,) + (1,) * (len(shape) - 1 - position))
    return gain


def split_up(count, total, most, skew):
    weights = [(1 << 20) // math.isqrt(grade ** skew) + 1 for grade in range(2, count + 1)]
    rest, counts = total - most - (count - 1), [1] * (count - 1)
    while rest > 0:
        movable = [i for i in range(count - 1) if counts[i] < most]
        pool, remaining = sum([weights[i] for i in movable]), rest
        for i in movable:
            extra = min(most - counts[i], max(1, remaining * weights[i] // pool), rest)
            counts[i] = counts[i] + extra
            rest = rest - extra
    return np.array([most] + counts)


def ragged_sizes(key, number_of, total, most, lean):
    if number_of == 2:
        one = jax.random.randint(key, (), max(1, total - most), min(most, total - 1) + 1)
        return jnp.stack([one, total - one])
    tallies = jnp.asarray(split_up(number_of, total, most, lean), jnp.int32)
    pairs = (number_of - 1) // 2
    giver, sink = tallies[1:1 + 2 * pairs:2], tallies[2:2 + 2 * pairs:2]
    room = jnp.minimum(giver - 1, most - sink)
    moved = jax.random.randint(jax.random.fold_in(key, 1), (pairs,), 0, 1 << 20) % (room + 1)
    tallies = tallies.at[1:1 + 2 * pairs:2].set(giver - moved).at[2:2 + 2 * pairs:2].set(sink + moved)
    return tallies[jax.random.permutation(jax.random.fold_in(key, 2), number_of)]


def routed_block(stream_key, own, number, rows, number_of, top, limit, skew):
    ranking = jax.random.permutation(stream_key, number_of)
    crowded, usual = portions_of(number_of, rows * top, limit, skew, True), portions_of(number_of, rows * top, limit, skew, False)
    places = jnp.arange(number_of)

    def named(tallies, turn):
        used = int((tallies > 0).sum())
        fixed = max(1, used // 4)
        passed = fixed + (places - fixed + turn * (used - fixed)) % max(1, number_of - fixed)
        return jnp.zeros((number_of,), jnp.int32).at[ranking[jnp.where(places < fixed, places, passed)]].set(jnp.asarray(tallies, jnp.int32))

    tallies = jnp.where(number % 4 == 0, named(crowded, number // 4), named(usual, number - number // 4 - 1))
    mixed = jax.random.permutation(jax.random.fold_in(own, 3), number_of)
    donor, taker = mixed[0:number_of // 2 * 2:2], mixed[1:number_of // 2 * 2:2]
    margin = jnp.minimum(tallies[donor] - 1, limit - tallies[taker]) // 2
    margin = jnp.where((donor == ranking[0]) | (taker == ranking[0]) | (tallies[taker] == 0), 0, jnp.maximum(margin, 0))
    passed = jax.random.randint(jax.random.fold_in(own, 4), (number_of // 2,), 0, 1 << 20) % (margin + 1)
    tallies = tallies.at[donor].add(-passed).at[taker].add(passed)
    members = jnp.searchsorted(jnp.cumsum(tallies), jnp.arange(rows * top), side="right").astype(jnp.int32)
    grid = members.reshape(top, rows).T
    grid = grid[jax.random.permutation(jax.random.fold_in(own, 1), rows)]
    turn = jax.random.randint(jax.random.fold_in(own, 2), (rows, 1), 0, top)
    return jnp.take_along_axis(grid, (jnp.arange(top)[None, :] + turn) % top, axis=1)


def portions_of(number_of, total, limit, slope, full):
    weights = [(1 << 20) // math.isqrt(grade ** slope) + 1 for grade in range(1, number_of + 1)]
    largest = limit if full else min(limit, max(-(-total // number_of), total * weights[0] // sum(weights)))
    least = 1 if total - largest >= number_of - 1 else 0
    counts, spare = [largest] + [least] * (number_of - 1), total - largest - least * (number_of - 1)
    while spare > 0:
        candidates = [i for i in range(1, number_of) if counts[i] < largest] or [i for i in range(1, number_of) if counts[i] < limit]
        pool, budget = sum([weights[i] for i in candidates]), spare
        for i in candidates:
            addition = min(limit - counts[i], max(1, budget * weights[i] // pool), spare)
            counts[i] = counts[i] + addition
            spare = spare - addition
    return np.array(counts)


def normal_values(stream_key, extent, scale, reach, cuts=(), kind=jnp.bfloat16):
    loudness = block_scale(stream_key, extent, cuts, -0.22, 0.18) if cuts else 1.0
    values = jax.random.normal(stream_key, extent, jnp.float32) * scale * loudness
    return jnp.minimum(jnp.maximum(values, -reach), reach).astype(kind)


def setup_inputs(seed: int = 0) -> dict:
    arg_keys = jax.random.split(jax.random.key(seed), 14)
    tokens = normal_values(arg_keys[0], (GROUPS, SEQ, MODEL_DIM), 1.0, 6.0, ((0, 8), (1, 4)))
    segment_ids = jax.vmap(lambda own: jnp.searchsorted(jnp.cumsum(ragged_sizes(own, SEGS, SEQ, SEQ - TOK_DEV + 1, 0)), jnp.arange(SEQ), side="right"))(jax.random.split(arg_keys[1], GROUPS)).reshape((GROUPS, SEQ)).astype(jnp.int32)
    routes_keys = jax.random.split(jax.random.fold_in(arg_keys[2], 1), GROUPS * SEQ // TOK_DEV)
    routes_turns = jax.random.permutation(jax.random.fold_in(arg_keys[2], 3), GROUPS * SEQ // TOK_DEV)
    routes = jax.vmap(lambda own, number: routed_block(jax.random.fold_in(arg_keys[2], 2), own, number, TOK_DEV, EXPERTS, TOP, CAP, 1))(routes_keys, routes_turns).reshape((GROUPS, SEQ, TOP))
    gain_attn = jnp.clip(1.0 + 0.1 * jax.random.normal(arg_keys[3], (MODEL_DIM,), jnp.float32), 0.5, 1.5).astype(jnp.bfloat16)
    w_query = normal_values(arg_keys[4], (MODEL_DIM, QUERY_HEADS * HEAD_SIZE), MODEL_DIM ** -0.5, 0.15625, ((0, 8),))
    key_weight = normal_values(arg_keys[5], (MODEL_DIM, KEY_VALUE_HEADS * HEAD_SIZE), MODEL_DIM ** -0.5, 0.15625, ((0, 8),))
    value_weight = normal_values(arg_keys[6], (MODEL_DIM, KEY_VALUE_HEADS * HEAD_SIZE), MODEL_DIM ** -0.5, 0.15625, ((0, 8),))
    w_out = normal_values(arg_keys[7], (QUERY_HEADS * HEAD_SIZE, MODEL_DIM), (QUERY_HEADS * HEAD_SIZE // 16) ** -0.5, 0.625, ((0, 8),))
    gain_ffn = jnp.clip(1.0 + 0.1 * jax.random.normal(arg_keys[8], (MODEL_DIM,), jnp.float32), 0.5, 1.5).astype(jnp.bfloat16)
    w_router = normal_values(arg_keys[9], (MODEL_DIM, EXPERTS), (4 * MODEL_DIM) ** -0.5, 0.078125, ((0, 8),))
    w_gate_up = normal_values(arg_keys[10], (MODEL_DIM, EXPERTS, 2 * FF), (MODEL_DIM // 4) ** -0.5, 0.3125, ((0, 8), (1, 4)))
    w_down = normal_values(arg_keys[11], (MODEL_DIM, EXPERTS, FF), (MODEL_DIM // 4) ** -0.5, 0.3125, ((0, 8), (1, 4)))
    cotangent = normal_values(arg_keys[12], (GROUPS, SEQ, MODEL_DIM), 1.0, 6.0, ((0, 8), (1, 4)))
    return dict(tokens=tokens, segment_ids=segment_ids, routes=routes, gain_attn=gain_attn, w_query=w_query, key_weight=key_weight, value_weight=value_weight, w_out=w_out, gain_ffn=gain_ffn, w_router=w_router, w_gate_up=w_gate_up, w_down=w_down, cotangent=cotangent)


epsilon = 1e-06
precise = lax.Precision.HIGHEST

@jax.custom_vjp
def reduced_input(v):
    return lax.optimization_barrier(v.astype(jnp.bfloat16)).astype(jnp.float32)

@jax.custom_vjp
def reduced_gradient(v):
    return v

def low_keep(v):
    return (reduced_input(v), None)

def low_pass(kept, grad):
    return (grad,)

def back_keep(v):
    return (v, None)

def back_low(kept, grad):
    return (reduced_input(grad),)
reduced_input.defvjp(low_keep, low_pass)
reduced_gradient.defvjp(back_keep, back_low)

def normalize(vector):
    return vector * lax.rsqrt(lax.optimization_barrier(jnp.mean(vector * vector, axis=-1, keepdims=True)) + epsilon)

def matrix_product(operand, other):
    return jnp.dot(operand, other, precision=precise)

def rope_tables(positions):
    freqs = 10000.0 ** (-(jnp.arange(HEAD_SIZE // 2, dtype=jnp.float32) * 2.0 / HEAD_SIZE))
    angles = positions.astype(jnp.float32)[:, None] * freqs[None, :]
    return (jnp.cos(angles), jnp.sin(angles))

def apply_rotary(vector, cosine_lookup, sine_lookup):
    half_size = HEAD_SIZE // 2
    front_half = vector[..., :half_size]
    back_half = vector[..., half_size:]
    cosine_wide = cosine_lookup[:, None, :]
    sine_wide = sine_lookup[:, None, :]
    return jnp.concatenate([front_half * cosine_wide - back_half * sine_wide, back_half * cosine_wide + front_half * sine_wide], -1)

def layer_group(inputs, segments, route_ids, gain_attn, w_query, key_weight, value_weight, w_out, gain_ffn, w_router, w_gate_up, w_down):
    document_length = inputs.shape[0]
    normed_one = normalize(inputs)
    normed_input_first = reduced_input(normed_one * gain_attn)
    query_rows = reduced_gradient(matrix_product(normed_input_first, w_query)).reshape(document_length, QUERY_HEADS, HEAD_SIZE)
    unrotated_keys = reduced_gradient(matrix_product(normed_input_first, key_weight)).reshape(document_length, KEY_VALUE_HEADS, HEAD_SIZE)
    value_rows = reduced_input(reduced_gradient(matrix_product(normed_input_first, value_weight))).reshape(document_length, KEY_VALUE_HEADS, HEAD_SIZE)
    positions = jnp.arange(document_length, dtype=jnp.int32)
    cosine_lookup, sine_lookup = rope_tables(positions)
    query_rows = reduced_input(apply_rotary(query_rows, cosine_lookup, sine_lookup)).reshape(document_length, KEY_VALUE_HEADS, QUERY_HEADS // KEY_VALUE_HEADS, HEAD_SIZE)
    keys_rot = reduced_input(apply_rotary(unrotated_keys, cosine_lookup, sine_lookup))
    block_rows = min(512, document_length)

    def attend(offset):
        query_block = lax.dynamic_slice_in_dim(query_rows, offset, block_rows, 0)
        scores = reduced_gradient(jnp.einsum('tjgd,sjd->jgts', query_block, keys_rot, precision=precise) * HEAD_SIZE ** (-0.5))
        query_pos = offset + jnp.arange(block_rows, dtype=jnp.int32)
        query_seg = lax.dynamic_slice_in_dim(segments, offset, block_rows, 0)
        allowed = (positions[None, :] <= query_pos[:, None]) & (segments[None, :] == query_seg[:, None])
        scores = jnp.where(allowed[None, None], scores, -1e+30)
        probs_low = reduced_input(jax.nn.softmax(scores, axis=-1))
        return jnp.einsum('jgts,sjd->tjgd', probs_low, value_rows, precision=precise)
    offsets = (jnp.arange(document_length // block_rows, dtype=jnp.int32) * block_rows).astype(jnp.int32)
    attended = lax.map(jax.checkpoint(attend), offsets).reshape(document_length, QUERY_HEADS * HEAD_SIZE)
    attended = reduced_input(reduced_gradient(attended))
    attn_branch = reduced_gradient(matrix_product(attended, w_out))
    hidden_one = inputs + attn_branch
    normed_two = normalize(hidden_one)
    xn_two = reduced_input(normed_two * gain_ffn)
    logits = reduced_gradient(matrix_product(xn_two, w_router))
    chosen = jnp.take_along_axis(logits, route_ids, axis=1)
    gate_weights = jax.nn.softmax(chosen, axis=-1)
    blocks = document_length // TOK_DEV
    flat_ids = route_ids.reshape(blocks, TOK_DEV * TOP)
    onehot = (flat_ids[..., None] == jnp.arange(EXPERTS, dtype=jnp.int32)).astype(jnp.int32)
    earlier = jnp.cumsum(onehot, axis=1) - onehot
    slot_ranks = lax.optimization_barrier(jnp.sum(earlier * onehot, axis=-1))
    slot_index = (flat_ids * (blocks * CAP) + jnp.arange(blocks, dtype=jnp.int32)[:, None] * CAP + slot_ranks).reshape(-1).astype(jnp.int32)
    route_rows = jnp.repeat(xn_two, TOP, axis=0)
    buffer = jnp.zeros((EXPERTS * blocks * CAP, MODEL_DIM), xn_two.dtype).at[slot_index].set(route_rows)
    buffer = reduced_gradient(buffer).reshape(EXPERTS, blocks * CAP, MODEL_DIM)
    gate_up_stack = jnp.transpose(w_gate_up, (1, 0, 2))
    down_stack = jnp.transpose(w_down, (1, 0, 2))

    def expert(operands):
        expert_rows, weight_in, weight_down = operands
        gate_up = reduced_gradient(matrix_product(expert_rows, weight_in))
        activated = reduced_input(reduced_gradient(jax.nn.silu(gate_up[:, :FF]) * gate_up[:, FF:]))
        return reduced_input(reduced_gradient(jnp.dot(activated, weight_down.T, precision=precise)))
    expert_out = lax.map(jax.checkpoint(expert), (buffer, gate_up_stack, down_stack)).reshape(-1, MODEL_DIM)
    routed = expert_out[slot_index].reshape(document_length, TOP, MODEL_DIM)
    return hidden_one + lax.optimization_barrier(jnp.sum(gate_weights[..., None] * routed, axis=1))

def forward(inputs, segment_ids, routes, *weights):

    def one_group(operands):
        group_inputs, group_segments, group_routes = operands
        return layer_group(group_inputs, group_segments, group_routes, *weights)
    return lax.map(jax.checkpoint(one_group), (inputs, segment_ids, routes))

def reference(tokens, segment_ids, routes, gain_attn, w_query, key_weight, value_weight, w_out, gain_ffn, w_router, w_gate_up, w_down, cotangent):
    weights = tuple((weight.astype(jnp.float32) for weight in (gain_attn, w_query, key_weight, value_weight, w_out, gain_ffn, w_router, w_gate_up, w_down)))

    def closed(inputs, *params):
        return forward(inputs, segment_ids, routes, *params)
    mixed, puller = jax.vjp(closed, tokens.astype(jnp.float32), *weights)
    grads = puller(cotangent.astype(jnp.float32))
    return (mixed.astype(jnp.bfloat16), grads[0].astype(jnp.bfloat16), grads[1], grads[2], grads[3], grads[4], grads[5], grads[6], grads[7], grads[8], grads[9])
```

```python
import functools

import jax
import jax.numpy as jnp
from jax import lax
from jax.experimental import pallas as pl
from jax.experimental.pallas import tpu as pltpu
from jax.sharding import PartitionSpec as P

QUERY_HEADS = 24
KEY_VALUE_HEADS = 8
GROUP = QUERY_HEADS // KEY_VALUE_HEADS
HEAD_SIZE = 64
HALF = HEAD_SIZE // 2
FF = 512
TOP = 8
EXP_DEV = 5
BLOCK = 256
MASKED = -1e30
epsilon = 1e-06


def dot(a, b, ca, cb):
    return lax.dot_general(a, b, (((ca,), (cb,)), ((), ())), preferred_element_type=jnp.float32)


def inverse_rms(v):
    return lax.rsqrt(jnp.mean(v * v, axis=-1, keepdims=True) + epsilon)


def allowed_tile(seg_col, seg_row, qi, ki):
    keys = seg_col[pl.ds(ki * BLOCK, BLOCK), :]
    queries = seg_row[:, pl.ds(qi * BLOCK, BLOCK)]
    ok = keys == queries
    if qi == ki:
        kpos = lax.broadcasted_iota(jnp.int32, (BLOCK, BLOCK), 0)
        qpos = lax.broadcasted_iota(jnp.int32, (BLOCK, BLOCK), 1)
        ok = ok & (kpos <= qpos)
    return ok


def attention_forward_kernel(blocks, q_ref, k_ref, v_ref, seg_col, seg_row, o_ref, lse_ref):
    keys = k_ref[0].astype(jnp.float32).T.astype(jnp.bfloat16)
    for qi in range(blocks):
        qs = slice(qi * BLOCK, (qi + 1) * BLOCK)
        q = q_ref[0, :, qs]
        top = total = acc = None
        for ki in range(qi, -1, -1):
            ks = slice(ki * BLOCK, (ki + 1) * BLOCK)
            s = dot(keys[ks, :], q, 1, 0)
            s = jnp.where(allowed_tile(seg_col, seg_row, qi, ki), s, MASKED)
            peak = jnp.max(s, axis=0, keepdims=True)
            if top is None:
                top = peak
                e = jnp.exp(s - top)
                total = jnp.sum(e, axis=0, keepdims=True)
                acc = dot(v_ref[0, :, ks], e.astype(jnp.bfloat16), 1, 0)
            else:
                new = jnp.maximum(top, peak)
                scale = jnp.exp(top - new)
                e = jnp.exp(s - new)
                total = total * scale + jnp.sum(e, axis=0, keepdims=True)
                acc = acc * scale + dot(v_ref[0, :, ks], e.astype(jnp.bfloat16), 1, 0)
                top = new
        o_ref[0, :, qs] = (acc / total).astype(jnp.bfloat16)
        lse_ref[0, :, qs] = top + jnp.log(total)


def attention_forward(q, k, v, seg):
    heads, _, length = q.shape
    blocks = length // BLOCK
    full = pl.BlockSpec((1, HEAD_SIZE, length), lambda h: (h, 0, 0))
    shared = pl.BlockSpec((1, HEAD_SIZE, length), lambda h: (h // GROUP, 0, 0))
    return pl.pallas_call(
        functools.partial(attention_forward_kernel, blocks),
        grid=(heads,),
        in_specs=[
            full,
            shared,
            shared,
            pl.BlockSpec((length, 1), lambda h: (0, 0)),
            pl.BlockSpec((1, length), lambda h: (0, 0)),
        ],
        out_specs=[full, pl.BlockSpec((1, 1, length), lambda h: (h, 0, 0))],
        out_shape=[
            jax.ShapeDtypeStruct((heads, HEAD_SIZE, length), jnp.bfloat16),
            jax.ShapeDtypeStruct((heads, 1, length), jnp.float32),
        ],
        compiler_params=pltpu.CompilerParams(vmem_limit_bytes=48 * 1024 * 1024),
        cost_estimate=pl.CostEstimate(
            flops=4 * heads * length * length * HEAD_SIZE,
            bytes_accessed=6 * heads * length * HEAD_SIZE,
            transcendentals=heads * length * length // 2,
        ),
        name="attention_forward",
    )(q, k, v, seg[:, None], seg[None, :])


def attention_backward_kernel(
    blocks, q_ref, k_ref, v_ref, o_ref, g_ref, lse_ref, seg_col, seg_row, dq_ref, dk_ref, dv_ref, dk_acc, dv_acc
):
    member = pl.program_id(1)

    @pl.when(member == 0)
    def _():
        dk_acc[...] = jnp.zeros_like(dk_acc)
        dv_acc[...] = jnp.zeros_like(dv_acc)

    keys_t = k_ref[0]
    keys = keys_t.astype(jnp.float32).T.astype(jnp.bfloat16)
    values = v_ref[0].astype(jnp.float32).T.astype(jnp.bfloat16)
    for qi in range(blocks):
        qs = slice(qi * BLOCK, (qi + 1) * BLOCK)
        q = q_ref[0, :, qs]
        g = g_ref[0, :, qs]
        g32 = g.astype(jnp.float32)
        delta = jnp.sum(g32 * o_ref[0, :, qs].astype(jnp.float32), axis=0, keepdims=True)
        lse = lse_ref[0, :, qs]
        q_rows = q.astype(jnp.float32).T.astype(jnp.bfloat16)
        g_rows = g32.T.astype(jnp.bfloat16)
        dq = jnp.zeros((HEAD_SIZE, BLOCK), jnp.float32)
        for ki in range(qi + 1):
            ks = slice(ki * BLOCK, (ki + 1) * BLOCK)
            s = dot(keys[ks, :], q, 1, 0)
            p = jnp.where(allowed_tile(seg_col, seg_row, qi, ki), jnp.exp(s - lse), 0.0)
            dp = dot(values[ks, :], g, 1, 0)
            ds = (p * (dp - delta)).astype(jnp.bfloat16)
            dv_acc[ks, :] += dot(p.astype(jnp.bfloat16), g_rows, 1, 0)
            dk_acc[ks, :] += dot(ds, q_rows, 1, 0)
            dq = dq + dot(keys_t[:, ks], ds, 1, 0)
        dq_ref[0, :, qs] = dq

    @pl.when(member == GROUP - 1)
    def _():
        dk_ref[0] = dk_acc[...].T
        dv_ref[0] = dv_acc[...].T


def attention_backward(q, k, v, o, g, lse, seg):
    heads, _, length = q.shape
    blocks = length // BLOCK
    full = pl.BlockSpec((1, HEAD_SIZE, length), lambda j, m: (j * GROUP + m, 0, 0))
    shared = pl.BlockSpec((1, HEAD_SIZE, length), lambda j, m: (j, 0, 0))
    return pl.pallas_call(
        functools.partial(attention_backward_kernel, blocks),
        grid=(heads // GROUP, GROUP),
        in_specs=[
            full,
            shared,
            shared,
            full,
            full,
            pl.BlockSpec((1, 1, length), lambda j, m: (j * GROUP + m, 0, 0)),
            pl.BlockSpec((length, 1), lambda j, m: (0, 0)),
            pl.BlockSpec((1, length), lambda j, m: (0, 0)),
        ],
        out_specs=[full, shared, shared],
        out_shape=[
            jax.ShapeDtypeStruct((heads, HEAD_SIZE, length), jnp.float32),
            jax.ShapeDtypeStruct((heads // GROUP, HEAD_SIZE, length), jnp.float32),
            jax.ShapeDtypeStruct((heads // GROUP, HEAD_SIZE, length), jnp.float32),
        ],
        scratch_shapes=[
            pltpu.VMEM((length, HEAD_SIZE), jnp.float32),
            pltpu.VMEM((length, HEAD_SIZE), jnp.float32),
        ],
        compiler_params=pltpu.CompilerParams(vmem_limit_bytes=48 * 1024 * 1024),
        cost_estimate=pl.CostEstimate(
            flops=10 * heads * length * length * HEAD_SIZE,
            bytes_accessed=16 * heads * length * HEAD_SIZE,
            transcendentals=heads * length * length // 2,
        ),
        name="attention_backward",
    )(q, k, v, o, g, lse, seg[:, None], seg[None, :])


def rope_tables(length):
    freqs = 10000.0 ** (-(jnp.arange(HALF, dtype=jnp.float32) * 2.0 / HEAD_SIZE))
    angles = freqs[:, None] * jnp.arange(length, dtype=jnp.float32)[None, :]
    return jnp.cos(angles)[None], jnp.sin(angles)[None]


def rotate(v, cosine, sine):
    a, b = v[:, :HALF, :], v[:, HALF:, :]
    return jnp.concatenate([a * cosine - b * sine, b * cosine + a * sine], axis=1)


def gather_expert(v):
    return lax.all_gather(v, "expert", axis=0, tiled=True)


def scatter_expert(v):
    return lax.psum_scatter(v, "expert", scatter_dimension=0, tiled=True)


def gather_shard(v):
    return lax.all_gather(v, "shard", axis=0, tiled=True)


def scatter_shard(v):
    return lax.psum_scatter(v, "shard", scatter_dimension=0, tiled=True)


def body(
    tokens,
    segment_ids,
    routes,
    gain_attn,
    w_query,
    key_weight,
    value_weight,
    w_out,
    gain_ffn,
    w_router,
    w_gate_up,
    w_down,
    cotangent,
):
    bf16, f32 = jnp.bfloat16, jnp.float32
    members = lax.axis_size("expert")
    shards = lax.axis_size("shard")
    me = lax.axis_index("expert")
    rows, width = tokens.shape[1:]
    length = rows * members
    shard_rows = w_query.shape[0]
    experts = EXP_DEV * members
    q_cols = QUERY_HEADS * HEAD_SIZE // members
    k_cols = KEY_VALUE_HEADS * HEAD_SIZE // members
    heads, kv_heads = q_cols // HEAD_SIZE, k_cols // HEAD_SIZE
    out_rows = width // (members * shards)

    def cols(w, n):
        return lax.dynamic_slice_in_dim(w, me * n, n, axis=1)

    first = jnp.concatenate(
        [cols(w_query, q_cols), cols(key_weight, k_cols), cols(value_weight, k_cols)], axis=1
    )
    small = jnp.concatenate([w_router, gain_attn[:, None], gain_ffn[:, None]], axis=1)
    full_small = gather_shard(small)
    full_qkv = gather_shard(first)
    full_router = full_small[:, :experts]
    gain_one = full_small[:, experts].astype(f32)
    gain_two = full_small[:, experts + 1].astype(f32)
    out_piece = cols(w_out, q_cols)
    full_out = jnp.concatenate(
        [
            lax.all_gather(gather_shard(out_piece), "expert", axis=0)[i]
            for i in range(members)
        ],
        axis=1,
    )
    pieces = [
        gather_shard(jnp.concatenate([w_gate_up[:, j, :], w_down[:, j, :]], axis=1))
        for j in range(EXP_DEV)
    ]

    all_tokens = gather_expert(tokens[0])
    meta = gather_expert(jnp.concatenate([segment_ids[0][:, None], routes[0]], axis=1))
    seg = meta[:, 0]
    route_ids = meta[:, 1:]
    all_grad = gather_expert(cotangent[0])

    inputs = all_tokens.astype(f32)
    normed_one = inputs * inverse_rms(inputs)
    xn_one = (normed_one * gain_one).astype(bf16)
    qkv = dot(full_qkv, xn_one, 0, 1).reshape(heads + 2 * kv_heads, HEAD_SIZE, length)
    cosine, sine = rope_tables(length)
    rotated = rotate(qkv[: heads + kv_heads], cosine, sine).astype(bf16)
    queries = rotated[:heads] * jnp.asarray(HEAD_SIZE**-0.5, bf16)
    keys = rotated[heads:]
    values = qkv[heads + kv_heads :].astype(bf16)
    attended, lse = attention_forward(queries, keys, values, seg)
    attended_rows = attended.reshape(q_cols, length)
    attended_all = gather_expert(attended_rows)

    hidden = inputs + dot(attended_all, full_out, 0, 0)
    normed_two = hidden * inverse_rms(hidden)
    xn_two = (normed_two * gain_two).astype(bf16)

    logits = jnp.dot(xn_two, full_router, preferred_element_type=f32)
    named = jnp.any(
        route_ids[:, :, None] == jnp.arange(experts, dtype=jnp.int32)[None, None, :], axis=1
    )
    peak = jnp.max(jnp.where(named, logits, -jnp.inf), axis=1, keepdims=True)
    exps = jnp.where(named, jnp.exp(jnp.minimum(logits - peak, 0.0)), 0.0)
    gates = exps / jnp.sum(exps, axis=1, keepdims=True)
    my_gates = lax.dynamic_slice_in_dim(gates, me * EXP_DEV, EXP_DEV, axis=1)

    xn_t, grad_t = xn_two.T, all_grad.T
    mix = jnp.zeros((length, width), f32)
    grad_in = jnp.zeros((length, width), f32)
    gate_grads, expert_grads = [], []
    for j in range(EXP_DEV):
        w_in, w_back = pieces[j][:, : 2 * FF], pieces[j][:, 2 * FF :]
        gate_up = dot(xn_two, w_in, 1, 0)
        through = dot(all_grad, w_back, 1, 0)
        gate, up = gate_up[:, :FF], gate_up[:, FF:]
        weight = my_gates[:, j : j + 1]
        sig = jax.nn.sigmoid(gate)
        act = gate * sig * up
        gate_grads.append(jnp.sum(act * through, axis=1, keepdims=True))
        scaled = (weight * act).astype(bf16)
        grad_act = weight * through
        back = jnp.concatenate(
            [grad_act * up * sig * (1.0 + gate * (1.0 - sig)), grad_act * gate * sig], axis=1
        ).astype(bf16)
        mix = mix + dot(scaled, w_back, 1, 1)
        grad_in = grad_in + dot(back, w_in, 1, 1)
        grads = jnp.concatenate([dot(xn_t, back, 1, 0), dot(grad_t, scaled, 1, 0)], axis=1)
        expert_grads.append(scatter_shard(grads.astype(bf16)))

    def mine(v):
        return lax.dynamic_slice_in_dim(v, me * rows, rows, axis=0)

    grad_gates = gather_expert(jnp.concatenate(gate_grads, axis=1).T).T
    grad_chosen = gates * (grad_gates - jnp.sum(gates * grad_gates, axis=1, keepdims=True))
    grad_logits = grad_chosen.astype(bf16)
    grad_xn_two = scatter_expert(grad_in.astype(bf16)).astype(f32)
    grad_xn_two = grad_xn_two + dot(mine(grad_logits), full_router, 1, 1)
    my_hidden = mine(hidden)
    mixed = (my_hidden + scatter_expert(mix.astype(bf16)).astype(f32)).astype(bf16)

    my_scale = inverse_rms(my_hidden)
    my_normed = my_hidden * my_scale
    grad_gain_two = jnp.sum(grad_xn_two * my_normed, axis=0)
    g = grad_xn_two * gain_two
    grad_hidden = cotangent[0].astype(f32) + my_scale * (
        g - my_normed * jnp.mean(g * my_normed, axis=-1, keepdims=True)
    )
    grad_attn = gather_expert(grad_hidden.astype(bf16))
    out_mine = lax.dynamic_slice_in_dim(full_out, me * q_cols, q_cols, axis=0)
    grad_attended = dot(out_mine, grad_attn, 1, 1).astype(bf16).reshape(heads, HEAD_SIZE, length)
    grad_out = jnp.dot(attended_rows, grad_attn, preferred_element_type=f32)
    grad_router = dot(cols(xn_two, q_cols), grad_logits, 0, 0)
    out_grads = scatter_shard(
        jnp.concatenate([grad_out, grad_router], axis=1).astype(bf16)
    ).astype(f32)

    dq, dk, dv = attention_backward(queries, keys, values, attended, grad_attended, lse, seg)
    dq = rotate(dq, cosine, -sine) * HEAD_SIZE**-0.5
    dk = rotate(dk, cosine, -sine)
    grad_qkv = jnp.concatenate([dq, dk, dv], axis=0).astype(bf16).reshape(-1, length)
    grad_first = dot(xn_one, grad_qkv, 0, 1)
    grad_xn_one = dot(grad_qkv, full_qkv, 0, 1)
    grad_xn_one = scatter_expert(grad_xn_one.astype(bf16)).astype(f32)
    my_inputs = tokens[0].astype(f32)
    scale_one = inverse_rms(my_inputs)
    normed = my_inputs * scale_one
    grad_gain_one = jnp.sum(grad_xn_one * normed, axis=0)
    h = grad_xn_one * gain_one
    grad_tokens = grad_hidden + scale_one * (h - normed * jnp.mean(h * normed, axis=-1, keepdims=True))

    total_cols = q_cols + 2 * k_cols
    grad_first = jnp.transpose(
        grad_first.astype(bf16).reshape(members, shards, out_rows, total_cols), (1, 0, 2, 3)
    ).reshape(width, total_cols)
    grad_first = scatter_shard(grad_first).reshape(members, out_rows, total_cols)
    grad_first = lax.all_to_all(grad_first, "expert", split_axis=0, concat_axis=0, tiled=True)
    grad_first = jnp.transpose(grad_first, (1, 0, 2)).astype(f32)
    gains = lax.psum_scatter(
        jnp.stack([grad_gain_one, grad_gain_two], axis=1),
        ("expert", "shard"),
        scatter_dimension=0,
        tiled=True,
    )
    expert_grads = jnp.stack(expert_grads, axis=1).astype(f32)
    return (
        mixed[None],
        grad_tokens.astype(bf16)[None],
        gains[:, 0],
        grad_first[:, :, :q_cols].reshape(out_rows, -1),
        grad_first[:, :, q_cols : q_cols + k_cols].reshape(out_rows, -1),
        grad_first[:, :, q_cols + k_cols :].reshape(out_rows, -1),
        out_grads[:, :width],
        gains[:, 1],
        out_grads[:, width:],
        expert_grads[:, :, : 2 * FF],
        expert_grads[:, :, 2 * FF :],
    )


def solution(mesh):
    in_specs = (
        P("shard", "expert", None),
        P("shard", "expert"),
        P("shard", "expert", None),
        P("shard"),
        P("shard", None),
        P("shard", None),
        P("shard", None),
        P("shard", None),
        P("shard"),
        P("shard", None),
        P("shard", "expert", None),
        P("shard", "expert", None),
        P("shard", "expert", None),
    )
    out_specs = (
        P("shard", "expert", None),
        P("shard", "expert", None),
        P(("expert", "shard")),
        P(("expert", "shard"), None),
        P(("expert", "shard"), None),
        P(("expert", "shard"), None),
        P(("expert", "shard"), None),
        P(("expert", "shard")),
        P(("expert", "shard"), None),
        P("shard", "expert", None),
        P("shard", "expert", None),
    )
    return jax.shard_map(body, mesh=mesh, in_specs=in_specs, out_specs=out_specs, check_vma=False)
```

```python
import functools

import jax
import jax.numpy as jnp
from jax import lax
from jax.experimental import pallas as pl
from jax.experimental.pallas import tpu as pltpu
from jax.sharding import PartitionSpec as P

QUERY_HEADS = 24
KEY_VALUE_HEADS = 8
GROUP = QUERY_HEADS // KEY_VALUE_HEADS
HEAD_SIZE = 64
HALF = HEAD_SIZE // 2
FF = 512
TOP = 8
EXP_DEV = 5
BLOCK = 256
CHUNKS = ((0, 1), (2, 3), (4,))
MASKED = -1e30
epsilon = 1e-06


def dot(a, b, ca, cb):
    return lax.dot_general(a, b, (((ca,), (cb,)), ((), ())), preferred_element_type=jnp.float32)


def inverse_rms(v):
    return lax.rsqrt(jnp.mean(v * v, axis=-1, keepdims=True) + epsilon)


def place_of(block, mine, members):
    r = block ^ mine
    return (r & 1) * (members // 2) + (r >> 1)


def spans(me_ref, blocks):
    return [pl.multiple_of(place_of(a, me_ref[0], blocks) * BLOCK, BLOCK) for a in range(blocks)]


def allowed_tile(seg_col, seg_row, at, qi, ki):
    ok = seg_col[pl.ds(at[ki], BLOCK), :] == seg_row[:, pl.ds(at[qi], BLOCK)]
    if qi == ki:
        kpos = lax.broadcasted_iota(jnp.int32, (BLOCK, BLOCK), 0)
        qpos = lax.broadcasted_iota(jnp.int32, (BLOCK, BLOCK), 1)
        ok = ok & (kpos <= qpos)
    return ok


def attention_forward_kernel(blocks, me_ref, q_ref, k_ref, v_ref, seg_col, seg_row, o_ref, lse_ref, keys):
    at = spans(me_ref, blocks)
    keys[...] = k_ref[0].astype(jnp.float32).T.astype(jnp.bfloat16)
    for qi in range(blocks):
        qs = pl.ds(at[qi], BLOCK)
        q = q_ref[0, :, qs]
        top = total = acc = None
        for ki in range(qi, -1, -1):
            ks = pl.ds(at[ki], BLOCK)
            s = dot(keys[ks, :], q, 1, 0)
            s = jnp.where(allowed_tile(seg_col, seg_row, at, qi, ki), s, MASKED)
            peak = jnp.max(s, axis=0, keepdims=True)
            if top is None:
                top = peak
                e = jnp.exp(s - top)
                total = jnp.sum(e, axis=0, keepdims=True)
                acc = dot(v_ref[0, :, ks], e.astype(jnp.bfloat16), 1, 0)
            else:
                new = jnp.maximum(top, peak)
                scale = jnp.exp(top - new)
                e = jnp.exp(s - new)
                total = total * scale + jnp.sum(e, axis=0, keepdims=True)
                acc = acc * scale + dot(v_ref[0, :, ks], e.astype(jnp.bfloat16), 1, 0)
                top = new
        o_ref[0, :, qs] = (acc / total).astype(jnp.bfloat16)
        lse_ref[0, :, qs] = top + jnp.log(total)


def attention_forward(me, q, k, v, seg):
    heads, _, length = q.shape
    blocks = length // BLOCK
    full = pl.BlockSpec((1, HEAD_SIZE, length), lambda h, me: (h, 0, 0))
    shared = pl.BlockSpec((1, HEAD_SIZE, length), lambda h, me: (h // GROUP, 0, 0))
    return pl.pallas_call(
        functools.partial(attention_forward_kernel, blocks),
        grid_spec=pltpu.PrefetchScalarGridSpec(
            num_scalar_prefetch=1,
            grid=(heads,),
            in_specs=[
                full,
                shared,
                shared,
                pl.BlockSpec((length, 1), lambda h, me: (0, 0)),
                pl.BlockSpec((1, length), lambda h, me: (0, 0)),
            ],
            out_specs=[full, pl.BlockSpec((1, 1, length), lambda h, me: (h, 0, 0))],
            scratch_shapes=[pltpu.VMEM((length, HEAD_SIZE), jnp.bfloat16)],
        ),
        out_shape=[
            jax.ShapeDtypeStruct((heads, HEAD_SIZE, length), jnp.bfloat16),
            jax.ShapeDtypeStruct((heads, 1, length), jnp.float32),
        ],
        compiler_params=pltpu.CompilerParams(vmem_limit_bytes=48 * 1024 * 1024),
        cost_estimate=pl.CostEstimate(
            flops=4 * heads * length * length * HEAD_SIZE,
            bytes_accessed=6 * heads * length * HEAD_SIZE,
            transcendentals=heads * length * length // 2,
        ),
        name="attention_forward",
    )(me, q, k, v, seg[:, None], seg[None, :])


def attention_backward_kernel(
    blocks, me_ref, q_ref, k_ref, v_ref, o_ref, g_ref, lse_ref, seg_col, seg_row,
    dq_ref, dk_ref, dv_ref, keys, values, dk_acc, dv_acc,
):
    at = spans(me_ref, blocks)
    member = pl.program_id(1)

    @pl.when(member == 0)
    def _():
        dk_acc[...] = jnp.zeros_like(dk_acc)
        dv_acc[...] = jnp.zeros_like(dv_acc)
        keys[...] = k_ref[0].astype(jnp.float32).T.astype(jnp.bfloat16)
        values[...] = v_ref[0].astype(jnp.float32).T.astype(jnp.bfloat16)

    for qi in range(blocks):
        qs = pl.ds(at[qi], BLOCK)
        q = q_ref[0, :, qs]
        g = g_ref[0, :, qs]
        g32 = g.astype(jnp.float32)
        delta = jnp.sum(g32 * o_ref[0, :, qs].astype(jnp.float32), axis=0, keepdims=True)
        lse = lse_ref[0, :, qs]
        q_rows = q.astype(jnp.float32).T.astype(jnp.bfloat16)
        g_rows = g32.T.astype(jnp.bfloat16)
        dq = jnp.zeros((HEAD_SIZE, BLOCK), jnp.float32)
        for ki in range(qi + 1):
            ks = pl.ds(at[ki], BLOCK)
            s = dot(keys[ks, :], q, 1, 0)
            p = jnp.where(allowed_tile(seg_col, seg_row, at, qi, ki), jnp.exp(s - lse), 0.0)
            dp = dot(values[ks, :], g, 1, 0)
            ds = (p * (dp - delta)).astype(jnp.bfloat16)
            dv_acc[ks, :] += dot(p.astype(jnp.bfloat16), g_rows, 1, 0)
            dk_acc[ks, :] += dot(ds, q_rows, 1, 0)
            dq = dq + dot(k_ref[0, :, ks], ds, 1, 0)
        dq_ref[0, :, qs] = dq

    @pl.when(member == GROUP - 1)
    def _():
        dk_ref[0] = dk_acc[...].T
        dv_ref[0] = dv_acc[...].T


def attention_backward(me, q, k, v, o, g, lse, seg):
    heads, _, length = q.shape
    blocks = length // BLOCK
    full = pl.BlockSpec((1, HEAD_SIZE, length), lambda j, m, me: (j * GROUP + m, 0, 0))
    shared = pl.BlockSpec((1, HEAD_SIZE, length), lambda j, m, me: (j, 0, 0))
    return pl.pallas_call(
        functools.partial(attention_backward_kernel, blocks),
        grid_spec=pltpu.PrefetchScalarGridSpec(
            num_scalar_prefetch=1,
            grid=(heads // GROUP, GROUP),
            in_specs=[
                full,
                shared,
                shared,
                full,
                full,
                pl.BlockSpec((1, 1, length), lambda j, m, me: (j * GROUP + m, 0, 0)),
                pl.BlockSpec((length, 1), lambda j, m, me: (0, 0)),
                pl.BlockSpec((1, length), lambda j, m, me: (0, 0)),
            ],
            out_specs=[full, shared, shared],
            scratch_shapes=[
                pltpu.VMEM((length, HEAD_SIZE), jnp.bfloat16),
                pltpu.VMEM((length, HEAD_SIZE), jnp.bfloat16),
                pltpu.VMEM((length, HEAD_SIZE), jnp.float32),
                pltpu.VMEM((length, HEAD_SIZE), jnp.float32),
            ],
        ),
        out_shape=[
            jax.ShapeDtypeStruct((heads, HEAD_SIZE, length), jnp.float32),
            jax.ShapeDtypeStruct((heads // GROUP, HEAD_SIZE, length), jnp.float32),
            jax.ShapeDtypeStruct((heads // GROUP, HEAD_SIZE, length), jnp.float32),
        ],
        compiler_params=pltpu.CompilerParams(vmem_limit_bytes=48 * 1024 * 1024),
        cost_estimate=pl.CostEstimate(
            flops=10 * heads * length * length * HEAD_SIZE,
            bytes_accessed=16 * heads * length * HEAD_SIZE,
            transcendentals=heads * length * length // 2,
        ),
        name="attention_backward",
    )(me, q, k, v, o, g, lse, seg[:, None], seg[None, :])


def rope_tables(positions):
    freqs = 10000.0 ** (-(jnp.arange(HALF, dtype=jnp.float32) * 2.0 / HEAD_SIZE))
    angles = freqs[:, None] * positions.astype(jnp.float32)[None, :]
    return jnp.cos(angles)[None], jnp.sin(angles)[None]


def rotate(v, cosine, sine):
    a, b = v[:, :HALF, :], v[:, HALF:, :]
    return jnp.concatenate([a * cosine - b * sine, b * cosine + a * sine], axis=1)


def swap_member(v, bit):
    n = lax.axis_size("expert")
    return lax.ppermute(v, "expert", [(i, i ^ bit) for i in range(n)])


def swap_shard(v):
    n = lax.axis_size("shard")
    return lax.ppermute(v, "shard", [(i, i ^ 1) for i in range(n)])


def swap_sequence(v):
    got = swap_shard(v[: v.shape[0] // 2])
    return jnp.concatenate([got, swap_member(got, 1)], axis=0)


def chip_bits():
    n = lax.axis_size("expert")
    return [1 << i for i in range(1, n.bit_length() - 1)]


def gather_members(v, axis=0):
    for bit in chip_bits() + [1]:
        v = jnp.concatenate([v, swap_member(v, bit)], axis=axis)
    return v


def gather_heads(v):
    members = lax.axis_size("expert")
    width = v.shape[1] // members
    for bit in chip_bits() + [1]:
        got = swap_member(v, bit)
        source = [place_of(2 * (p % (members // 2)) + p // (members // 2), bit, members) for p in range(members)]
        got = jnp.concatenate([got[:, p * width : (p + 1) * width] for p in source], axis=1)
        v = jnp.concatenate([v, got], axis=0)
    return v


def halves(v, axis):
    return jnp.split(v, 2, axis=axis)


def add_swapped(keep, sent, swap):
    return keep.astype(jnp.float32) + swap(sent).astype(jnp.float32)


def scatter_members(own, other, axis=0):
    kind = own.dtype
    parts = []
    for v in (own, other):
        keep, sent = halves(v, axis)
        parts.append(add_swapped(keep, sent, lambda u: swap_member(u, 1)).astype(kind))
    own, other = parts
    total = add_swapped(own, other, swap_shard)
    for bit in reversed(chip_bits()):
        keep, sent = halves(total.astype(kind), axis)
        total = add_swapped(keep, sent, lambda u: swap_member(u, bit))
    return total


def turn(first, back=False):
    members, shards = lax.axis_size("expert"), lax.axis_size("shard")
    pairs = []
    for e in range(members):
        for s in range(shards):
            core, low = e & 1, s & 1
            to_core, to_low = (low, core) if first else (1 - low, core)
            target = ((e & ~1) | to_core) * shards + ((s & ~1) | to_low)
            pairs.append((e * shards + s, target))
    if back:
        pairs = [(b, a) for a, b in pairs]
    return pairs


def permute_all(v, pairs):
    return lax.ppermute(v, ("expert", "shard"), pairs)


def shard_lines():
    n = lax.axis_size("shard")
    return [[s for s in range(n) if s & 1 == low] for low in range(2)]


def gather_shard(v):
    return lax.all_gather(v, "shard", axis=0, tiled=True)


def scatter_shard(v):
    return lax.psum_scatter(v, "shard", scatter_dimension=0, tiled=True)


def out_kernel(members, me_ref, slice_ref, out_ref):
    size = slice_ref.shape[2]
    p = pl.program_id(0)
    r = 2 * (p % (members // 2)) + p // (members // 2)
    col = pl.multiple_of((me_ref[0] ^ r) * size, 128)
    for a in range(members):
        row = pl.multiple_of(place_of(a, me_ref[0], members) * size, 16)
        out_ref[pl.ds(row, size), pl.ds(col, size)] = slice_ref[0, a * size : (a + 1) * size, :]


def assemble_out(me, slices):
    members, rows, size = slices.shape
    return pl.pallas_call(
        functools.partial(out_kernel, members),
        grid_spec=pltpu.PrefetchScalarGridSpec(
            num_scalar_prefetch=1,
            grid=(members,),
            in_specs=[pl.BlockSpec((1, rows, size), lambda p, me: (p, 0, 0))],
            out_specs=pl.BlockSpec((rows, size * members), lambda p, me: (0, 0)),
        ),
        out_shape=jax.ShapeDtypeStruct((rows, size * members), slices.dtype),
        compiler_params=pltpu.CompilerParams(vmem_limit_bytes=48 * 1024 * 1024),
        name="assemble_out",
    )(me, slices)


def body(
    tokens,
    segment_ids,
    routes,
    gain_attn,
    w_query,
    key_weight,
    value_weight,
    w_out,
    gain_ffn,
    w_router,
    w_gate_up,
    w_down,
    cotangent,
):
    bf16, f32 = jnp.bfloat16, jnp.float32
    members = lax.axis_size("expert")
    shards = lax.axis_size("shard")
    me = lax.axis_index("expert")
    core = me & 1
    low = lax.axis_index("shard") & 1
    rows, width = tokens.shape[1:]
    length = rows * members
    experts = EXP_DEV * members
    q_cols = QUERY_HEADS * HEAD_SIZE // members
    k_cols = KEY_VALUE_HEADS * HEAD_SIZE // members
    heads, kv_heads = q_cols // HEAD_SIZE, k_cols // HEAD_SIZE
    out_rows = width // (members * shards)
    half = FF // 2
    me_ref = me[None].astype(jnp.int32)

    def cols(w, n):
        return lax.dynamic_slice_in_dim(w, me * n, n, axis=1)

    small = jnp.concatenate([w_router, gain_attn[:, None], gain_ffn[:, None]], axis=1)
    total_cols = q_cols + 2 * k_cols
    first = jnp.concatenate(
        [
            cols(w_query, q_cols),
            cols(key_weight, k_cols),
            cols(value_weight, k_cols),
            cols(w_out, q_cols),
            jnp.pad(small, ((0, 0), (0, 128 - small.shape[1]))),
        ],
        axis=1,
    )
    first = gather_shard(first)
    full_qkv = first[:, :total_cols]
    out_slice = first[:, total_cols : total_cols + q_cols]
    full_small = first[:, total_cols + q_cols :]
    full_router = full_small[:, :experts]
    gain_one = full_small[:, experts].astype(f32)
    gain_two = full_small[:, experts + 1].astype(f32)

    all_tokens = gather_members(tokens[0])
    meta = gather_members(jnp.concatenate([segment_ids[0][:, None], routes[0]], axis=1))
    seg = meta[:, 0]
    my_routes = meta[:, 1:]
    route_ids = jnp.concatenate([my_routes, swap_shard(my_routes)], axis=0)
    my_grad = gather_members(cotangent[0])
    all_grad = jnp.concatenate([my_grad, swap_sequence(my_grad)], axis=0)

    weights = []
    for js in CHUNKS:
        sides = [
            jnp.concatenate(
                [w_gate_up[:, j, h * half : (h + 1) * half] for j in js]
                + [w_gate_up[:, j, FF + h * half : FF + (h + 1) * half] for j in js]
                + [w_down[:, j, h * half : (h + 1) * half] for j in js],
                axis=1,
            )
            for h in range(2)
        ]
        one = permute_all(jnp.where(low == 0, sides[0], sides[1]), turn(True))
        two = permute_all(jnp.where(low == 0, sides[1], sides[0]), turn(False))
        block = jnp.concatenate(
            [jnp.where(core == 0, one, two), jnp.where(core == 0, two, one)], axis=0
        )
        weights.append(
            lax.all_gather(block, "shard", axis=0, tiled=True, axis_index_groups=shard_lines())
        )

    inputs = all_tokens.astype(f32)
    normed_one = inputs * inverse_rms(inputs)
    xn_one = (normed_one * gain_one).astype(bf16)
    qkv = dot(full_qkv, xn_one, 0, 1).reshape(heads + 2 * kv_heads, HEAD_SIZE, length)
    order = jnp.arange(members, dtype=jnp.int32)
    order = me ^ (2 * (order % (members // 2)) + order // (members // 2))
    positions = (order[:, None] * rows + jnp.arange(rows, dtype=jnp.int32)[None, :]).reshape(-1)
    cosine, sine = rope_tables(positions)
    rotated = rotate(qkv[: heads + kv_heads], cosine, sine).astype(bf16)
    queries = rotated[:heads] * jnp.asarray(HEAD_SIZE**-0.5, bf16)
    keys = rotated[heads:]
    values = qkv[heads + kv_heads :].astype(bf16)
    attended, lse = attention_forward(me_ref, queries, keys, values, seg)
    attended_rows = attended.reshape(q_cols, length)
    attended_all = gather_heads(attended_rows)
    full_out = assemble_out(me_ref, gather_members(out_slice[None]))

    hidden = inputs + dot(attended_all, full_out, 0, 0)
    normed_two = hidden * inverse_rms(hidden)
    my_xn_two = (normed_two * gain_two).astype(bf16)
    xn_two = jnp.concatenate([my_xn_two, swap_sequence(my_xn_two)], axis=0)

    logits = jnp.dot(xn_two, full_router, preferred_element_type=f32)
    named = jnp.any(
        route_ids[:, :, None] == jnp.arange(experts, dtype=jnp.int32)[None, None, :], axis=1
    )
    peak = jnp.max(jnp.where(named, logits, -jnp.inf), axis=1, keepdims=True)
    exps = jnp.where(named, jnp.exp(jnp.minimum(logits - peak, 0.0)), 0.0)
    gates = exps / jnp.sum(exps, axis=1, keepdims=True)
    group = (me & ~1) | low
    my_gates = lax.dynamic_slice_in_dim(gates, group * EXP_DEV, EXP_DEV, axis=1)

    count = 2 * length
    mix = jnp.zeros((count, width), f32)
    grad_in = jnp.zeros((count, width), f32)
    gate_grads, expert_grads = [], []
    for js, w in zip(CHUNKS, weights):
        n = len(js) * half
        w_in, w_back = w[:, : 2 * n], w[:, 2 * n :]
        gate_up = dot(xn_two, w_in, 1, 0)
        through = dot(all_grad, w_back, 1, 0)
        gate, up = gate_up[:, :n], gate_up[:, n:]
        weight = jnp.concatenate(
            [jnp.broadcast_to(my_gates[:, j : j + 1], (count, half)) for j in js], axis=1
        )
        sig = jax.nn.sigmoid(gate)
        act = gate * sig * up
        product = act * through
        for i in range(len(js)):
            gate_grads.append(jnp.sum(product[:, i * half : (i + 1) * half], axis=1))
        scaled = (weight * act).astype(bf16)
        grad_act = weight * through
        back = jnp.concatenate(
            [grad_act * up * sig * (1.0 + gate * (1.0 - sig)), grad_act * gate * sig], axis=1
        ).astype(bf16)
        mix = mix + dot(scaled, w_back, 1, 1)
        grad_in = grad_in + dot(back, w_in, 1, 1)
        grads = jnp.concatenate([dot(xn_two, back, 0, 0), dot(all_grad, scaled, 0, 0)], axis=1)
        expert_grads.append(
            lax.psum_scatter(
                grads.astype(bf16),
                "shard",
                scatter_dimension=0,
                tiled=True,
                axis_index_groups=shard_lines(),
            )
        )

    grad_xn_two = scatter_members(grad_in[:length].astype(bf16), grad_in[length:].astype(bf16))
    gate_grads = lax.dynamic_update_slice_in_dim(
        jnp.zeros((experts, count), f32), jnp.stack(gate_grads, axis=0), group * EXP_DEV, axis=0
    )
    grad_gates = scatter_members(gate_grads[:, :length], gate_grads[:, length:], axis=1).T
    own_gates = gates[:rows]
    grad_chosen = own_gates * (grad_gates - jnp.sum(own_gates * grad_gates, axis=1, keepdims=True))
    grad_logits = grad_chosen.astype(bf16)
    grad_xn_two = grad_xn_two + dot(grad_logits, full_router, 1, 1)
    my_hidden = hidden[:rows]

    my_scale = inverse_rms(my_hidden)
    my_normed = my_hidden * my_scale
    grad_gain_two = jnp.sum(grad_xn_two * my_normed, axis=0)
    g = grad_xn_two * gain_two
    grad_hidden = cotangent[0].astype(f32) + my_scale * (
        g - my_normed * jnp.mean(g * my_normed, axis=-1, keepdims=True)
    )
    grad_attn = gather_members(grad_hidden.astype(bf16))
    grad_attended = dot(full_out[:q_cols], grad_attn, 1, 1).astype(bf16)
    grad_attended = grad_attended.reshape(heads, HEAD_SIZE, length)
    grad_out = jnp.dot(attended_rows, grad_attn, preferred_element_type=f32)
    out_grads = scatter_shard(grad_out.astype(bf16)).astype(f32)
    grad_router = dot(xn_two[:rows], grad_logits, 0, 0)

    dq, dk, dv = attention_backward(me_ref, queries, keys, values, attended, grad_attended, lse, seg)
    dq = rotate(dq, cosine, -sine) * HEAD_SIZE**-0.5
    dk = rotate(dk, cosine, -sine)
    grad_qkv = jnp.concatenate([dq, dk, dv], axis=0).astype(bf16).reshape(-1, length)
    grad_first = dot(xn_one, grad_qkv, 0, 1)
    grad_xn_one = dot(grad_qkv, full_qkv, 0, 1)
    grad_gain_one = jnp.sum(grad_xn_one * normed_one, axis=0)
    grad_xn_one = grad_xn_one.astype(bf16)
    for bit in [1] + chip_bits()[::-1]:
        keep, sent = halves(grad_xn_one.astype(bf16), 0)
        grad_xn_one = add_swapped(keep, sent, lambda u: swap_member(u, bit))
    my_inputs = tokens[0].astype(f32)
    scale_one = inverse_rms(my_inputs)
    normed = my_inputs * scale_one
    h = grad_xn_one * gain_one
    grad_tokens = grad_hidden + scale_one * (h - normed * jnp.mean(h * normed, axis=-1, keepdims=True))

    rest = jnp.concatenate([grad_router, grad_gain_one[:, None], grad_gain_two[:, None]], axis=1)
    rest = jnp.pad(rest, ((0, 0), (0, 128 - rest.shape[1])))
    grad_first = jnp.concatenate([grad_first, rest], axis=1).astype(bf16)
    grad_first = jnp.transpose(grad_first.reshape(members, shards, out_rows, -1), (1, 0, 2, 3))
    grad_first = scatter_shard(grad_first.reshape(width, -1)).reshape(members, out_rows, -1)
    grad_first = lax.all_to_all(grad_first, "expert", split_axis=0, concat_axis=0, tiled=True)
    rest = jnp.sum(grad_first[:, :, total_cols:].astype(f32), axis=0)
    grad_first = jnp.transpose(grad_first, (1, 0, 2)).astype(f32)

    mixed = my_hidden + scatter_members(mix[:length].astype(bf16), mix[length:].astype(bf16))

    gate_up_out, down_out = [], []
    for js, v in zip(CHUNKS, expert_grads):
        size = v.shape[0] // 2
        one = permute_all(jnp.where(core == 0, v[:size], v[size:]), turn(True, True))
        two = permute_all(jnp.where(core == 0, v[size:], v[:size]), turn(False, True))
        sides = [jnp.where(low == 0, one, two), jnp.where(low == 0, two, one)]
        n = len(js)
        for i in range(n):
            piece = [
                [sides[h][:, (k * n + i) * half : (k * n + i + 1) * half] for h in range(2)]
                for k in range(3)
            ]
            gate_up_out.append(jnp.concatenate(piece[0] + piece[1], axis=1))
            down_out.append(jnp.concatenate(piece[2], axis=1))
    return (
        mixed.astype(bf16)[None],
        grad_tokens.astype(bf16)[None],
        rest[:, experts],
        grad_first[:, :, :q_cols].reshape(out_rows, -1),
        grad_first[:, :, q_cols : q_cols + k_cols].reshape(out_rows, -1),
        grad_first[:, :, q_cols + k_cols : total_cols].reshape(out_rows, -1),
        out_grads,
        rest[:, experts + 1],
        rest[:, :experts],
        jnp.stack(gate_up_out, axis=1).astype(f32),
        jnp.stack(down_out, axis=1).astype(f32),
    )


def solution(mesh):
    in_specs = (
        P("shard", "expert", None),
        P("shard", "expert"),
        P("shard", "expert", None),
        P("shard"),
        P("shard", None),
        P("shard", None),
        P("shard", None),
        P("shard", None),
        P("shard"),
        P("shard", None),
        P("shard", "expert", None),
        P("shard", "expert", None),
        P("shard", "expert", None),
    )
    out_specs = (
        P("shard", "expert", None),
        P("shard", "expert", None),
        P(("expert", "shard")),
        P(("expert", "shard"), None),
        P(("expert", "shard"), None),
        P(("expert", "shard"), None),
        P(("expert", "shard"), None),
        P(("expert", "shard")),
        P(("expert", "shard"), None),
        P("shard", "expert", None),
        P("shard", "expert", None),
    )
    return jax.shard_map(body, mesh=mesh, in_specs=in_specs, out_specs=out_specs, check_vma=False)
```

```python
import functools

import jax
import jax.numpy as jnp
from jax import lax
from jax.experimental import pallas as pl
from jax.experimental.pallas import tpu as pltpu
from jax.sharding import PartitionSpec as P

QUERY_HEADS = 24
KEY_VALUE_HEADS = 8
GROUP = QUERY_HEADS // KEY_VALUE_HEADS
HEAD_SIZE = 64
HALF = HEAD_SIZE // 2
FF = 512
TOP = 8
EXP_DEV = 5
BLOCK = 256
TILE = 512
BANDS = 4
MASKED = -1e30
epsilon = 1e-06


def dot(a, b, ca, cb):
    return lax.dot_general(a, b, (((ca,), (cb,)), ((), ())), preferred_element_type=jnp.float32)


def inverse_rms(v):
    return lax.rsqrt(jnp.mean(v * v, axis=-1, keepdims=True) + epsilon)


def place_of(block, mine, members):
    r = block ^ mine
    return (r & 1) * (members // 2) + (r >> 1)


def spans(me_ref, blocks):
    return [pl.multiple_of(place_of(a, me_ref[0], blocks) * BLOCK, BLOCK) for a in range(blocks)]


def allowed_tile(seg_col, seg_row, at, qi, ki):
    ok = seg_col[pl.ds(at[ki], BLOCK), :] == seg_row[:, pl.ds(at[qi], BLOCK)]
    if qi == ki:
        kpos = lax.broadcasted_iota(jnp.int32, (BLOCK, BLOCK), 0)
        qpos = lax.broadcasted_iota(jnp.int32, (BLOCK, BLOCK), 1)
        ok = ok & (kpos <= qpos)
    return ok


def attention_forward_kernel(blocks, me_ref, q_ref, k_ref, v_ref, seg_col, seg_row, o_ref, lse_ref, keys):
    at = spans(me_ref, blocks)
    keys[...] = k_ref[0].astype(jnp.float32).T.astype(jnp.bfloat16)
    for qi in range(blocks):
        qs = pl.ds(at[qi], BLOCK)
        q = q_ref[0, :, qs]
        top = total = acc = None
        for ki in range(qi, -1, -1):
            ks = pl.ds(at[ki], BLOCK)
            s = dot(keys[ks, :], q, 1, 0)
            s = jnp.where(allowed_tile(seg_col, seg_row, at, qi, ki), s, MASKED)
            peak = jnp.max(s, axis=0, keepdims=True)
            if top is None:
                top = peak
                e = jnp.exp(s - top)
                total = jnp.sum(e, axis=0, keepdims=True)
                acc = dot(v_ref[0, :, ks], e.astype(jnp.bfloat16), 1, 0)
            else:
                new = jnp.maximum(top, peak)
                scale = jnp.exp(top - new)
                e = jnp.exp(s - new)
                total = total * scale + jnp.sum(e, axis=0, keepdims=True)
                acc = acc * scale + dot(v_ref[0, :, ks], e.astype(jnp.bfloat16), 1, 0)
                top = new
        o_ref[0, :, qs] = (acc / total).astype(jnp.bfloat16)
        lse_ref[0, :, qs] = top + jnp.log(total)


def attention_forward(me, q, k, v, seg):
    heads, _, length = q.shape
    blocks = length // BLOCK
    full = pl.BlockSpec((1, HEAD_SIZE, length), lambda h, me: (h, 0, 0))
    shared = pl.BlockSpec((1, HEAD_SIZE, length), lambda h, me: (h // GROUP, 0, 0))
    return pl.pallas_call(
        functools.partial(attention_forward_kernel, blocks),
        grid_spec=pltpu.PrefetchScalarGridSpec(
            num_scalar_prefetch=1,
            grid=(heads,),
            in_specs=[
                full,
                shared,
                shared,
                pl.BlockSpec((length, 1), lambda h, me: (0, 0)),
                pl.BlockSpec((1, length), lambda h, me: (0, 0)),
            ],
            out_specs=[full, pl.BlockSpec((1, 1, length), lambda h, me: (h, 0, 0))],
            scratch_shapes=[pltpu.VMEM((length, HEAD_SIZE), jnp.bfloat16)],
        ),
        out_shape=[
            jax.ShapeDtypeStruct((heads, HEAD_SIZE, length), jnp.bfloat16),
            jax.ShapeDtypeStruct((heads, 1, length), jnp.float32),
        ],
        compiler_params=pltpu.CompilerParams(vmem_limit_bytes=48 * 1024 * 1024),
        cost_estimate=pl.CostEstimate(
            flops=4 * heads * length * length * HEAD_SIZE,
            bytes_accessed=6 * heads * length * HEAD_SIZE,
            transcendentals=heads * length * length // 2,
        ),
        name="attention_forward",
    )(me, q, k, v, seg[:, None], seg[None, :])


def attention_backward_kernel(
    blocks, me_ref, q_ref, k_ref, v_ref, o_ref, g_ref, lse_ref, seg_col, seg_row,
    dq_ref, dk_ref, dv_ref, keys, values, dk_acc, dv_acc,
):
    at = spans(me_ref, blocks)
    member = pl.program_id(1)

    @pl.when(member == 0)
    def _():
        dk_acc[...] = jnp.zeros_like(dk_acc)
        dv_acc[...] = jnp.zeros_like(dv_acc)
        keys[...] = k_ref[0].astype(jnp.float32).T.astype(jnp.bfloat16)
        values[...] = v_ref[0].astype(jnp.float32).T.astype(jnp.bfloat16)

    for qi in range(blocks):
        qs = pl.ds(at[qi], BLOCK)
        q = q_ref[0, :, qs]
        g = g_ref[0, :, qs]
        g32 = g.astype(jnp.float32)
        delta = jnp.sum(g32 * o_ref[0, :, qs].astype(jnp.float32), axis=0, keepdims=True)
        lse = lse_ref[0, :, qs]
        q_rows = q.astype(jnp.float32).T.astype(jnp.bfloat16)
        g_rows = g32.T.astype(jnp.bfloat16)
        dq = jnp.zeros((HEAD_SIZE, BLOCK), jnp.float32)
        for ki in range(qi + 1):
            ks = pl.ds(at[ki], BLOCK)
            s = dot(keys[ks, :], q, 1, 0)
            p = jnp.where(allowed_tile(seg_col, seg_row, at, qi, ki), jnp.exp(s - lse), 0.0)
            dp = dot(values[ks, :], g, 1, 0)
            ds = (p * (dp - delta)).astype(jnp.bfloat16)
            dv_acc[ks, :] += dot(p.astype(jnp.bfloat16), g_rows, 1, 0)
            dk_acc[ks, :] += dot(ds, q_rows, 1, 0)
            dq = dq + dot(k_ref[0, :, ks], ds, 1, 0)
        dq_ref[0, :, qs] = dq

    @pl.when(member == GROUP - 1)
    def _():
        dk_ref[0] = dk_acc[...].T
        dv_ref[0] = dv_acc[...].T


def attention_backward(me, q, k, v, o, g, lse, seg):
    heads, _, length = q.shape
    blocks = length // BLOCK
    full = pl.BlockSpec((1, HEAD_SIZE, length), lambda j, m, me: (j * GROUP + m, 0, 0))
    shared = pl.BlockSpec((1, HEAD_SIZE, length), lambda j, m, me: (j, 0, 0))
    return pl.pallas_call(
        functools.partial(attention_backward_kernel, blocks),
        grid_spec=pltpu.PrefetchScalarGridSpec(
            num_scalar_prefetch=1,
            grid=(heads // GROUP, GROUP),
            in_specs=[
                full,
                shared,
                shared,
                full,
                full,
                pl.BlockSpec((1, 1, length), lambda j, m, me: (j * GROUP + m, 0, 0)),
                pl.BlockSpec((length, 1), lambda j, m, me: (0, 0)),
                pl.BlockSpec((1, length), lambda j, m, me: (0, 0)),
            ],
            out_specs=[full, shared, shared],
            scratch_shapes=[
                pltpu.VMEM((length, HEAD_SIZE), jnp.bfloat16),
                pltpu.VMEM((length, HEAD_SIZE), jnp.bfloat16),
                pltpu.VMEM((length, HEAD_SIZE), jnp.float32),
                pltpu.VMEM((length, HEAD_SIZE), jnp.float32),
            ],
        ),
        out_shape=[
            jax.ShapeDtypeStruct((heads, HEAD_SIZE, length), jnp.float32),
            jax.ShapeDtypeStruct((heads // GROUP, HEAD_SIZE, length), jnp.float32),
            jax.ShapeDtypeStruct((heads // GROUP, HEAD_SIZE, length), jnp.float32),
        ],
        compiler_params=pltpu.CompilerParams(vmem_limit_bytes=48 * 1024 * 1024),
        cost_estimate=pl.CostEstimate(
            flops=10 * heads * length * length * HEAD_SIZE,
            bytes_accessed=16 * heads * length * HEAD_SIZE,
            transcendentals=heads * length * length // 2,
        ),
        name="attention_backward",
    )(me, q, k, v, o, g, lse, seg[:, None], seg[None, :])


def rope_tables(positions):
    freqs = 10000.0 ** (-(jnp.arange(HALF, dtype=jnp.float32) * 2.0 / HEAD_SIZE))
    angles = freqs[:, None] * positions.astype(jnp.float32)[None, :]
    return jnp.cos(angles)[None], jnp.sin(angles)[None]


def rotate(v, cosine, sine):
    a, b = v[:, :HALF, :], v[:, HALF:, :]
    return jnp.concatenate([a * cosine - b * sine, b * cosine + a * sine], axis=1)


def side_tiles(tiles):
    return [(0, tiles // 2), (tiles // 2, tiles // 4), (3 * tiles // 4, tiles // 4)]


def expert_kernel(start, n, half, tiles, band, has_in, parts, *refs):
    refs = list(refs)
    x_refs = refs[:3]
    g_refs = refs[3:6]
    wt_refs = refs[6:8]
    w_ref = refs[8]
    refs = refs[9:]
    gin_in = refs.pop(0) if has_in else None
    gin_refs, refs = refs[:parts], refs[parts:]
    s_ref, gg_ref, dw_ref, xs, gs, ss, bs, sems = refs
    step = pl.program_id(0)
    later = step - tiles
    m = 2 * n * half
    arrivals = []
    for side, (first, size) in enumerate(side_tiles(tiles)):
        for i in range(size):
            to = slice((first + i) * TILE, (first + i + 1) * TILE)
            arrivals.append(
                [
                    pltpu.make_async_copy(
                        sources[side].at[slice(i * TILE, (i + 1) * TILE), :],
                        target.at[to, :],
                        sems.at[k, first + i],
                    )
                    for k, (sources, target) in enumerate(((x_refs, xs), (g_refs, gs)))
                ]
            )

    @pl.when(step == 0)
    def _():
        for pair in arrivals:
            for copy in pair:
                copy.start()

    for i, pair in enumerate(arrivals):

        @pl.when(step == i)
        def _():
            for copy in pair:
                copy.wait()

    @pl.when(step < tiles)
    def _():
        at = pl.ds(pl.multiple_of(step * TILE, TILE), TILE)
        x = xs[at, :]
        g = gs[at, :]
        weights = jnp.where(step < tiles // 2, wt_refs[0][...], wt_refs[1][...]).T
        sums = []
        for i in range(n):
            c = [slice((k * n + i) * half, (k * n + i + 1) * half) for k in range(3)]
            gate = dot(x, w_ref[:, c[0]], 1, 0)
            up = dot(x, w_ref[:, c[1]], 1, 0)
            through = dot(g, w_ref[:, c[2]], 1, 0)
            weight = weights[:, start + i : start + i + 1]
            sig = jax.nn.sigmoid(gate)
            soft = gate * sig
            act = soft * up
            sums.append(jnp.sum(act * through, axis=1, keepdims=True))
            scaled = (weight * act).astype(jnp.bfloat16)
            ss[at, c[0]] = scaled
            s_ref[:, c[0]] = scaled
            grad = weight * through
            bs[at, c[0]] = (grad * up * sig * (1.0 + gate * (1.0 - sig))).astype(jnp.bfloat16)
            bs[at, c[1]] = (grad * soft).astype(jnp.bfloat16)
        gg_ref[...] = jnp.concatenate(sums, axis=1).T

    @pl.when(later >= 0)
    def _():
        tile = tiles - 1 - later
        at = pl.ds(pl.multiple_of(tile * TILE, TILE), TILE)
        gin = dot(bs[at, :], w_ref[:, :m], 1, 1)
        if has_in:
            gin = gin + gin_in[...]
        if parts == 1:
            gin_refs[0][...] = gin
        else:
            for part in range(parts):

                @pl.when(tile * parts // tiles == part)
                def _():
                    gin_refs[part][...] = gin.astype(jnp.bfloat16)

    @pl.when((later >= 0) & (later < BANDS))
    def _():
        at = pl.ds(pl.multiple_of(later * band, band), band)
        dw_ref[:, :m] = dot(xs[:, at], bs[...], 0, 0).astype(jnp.bfloat16)
        dw_ref[:, m:] = dot(gs[:, at], ss[...], 0, 0).astype(jnp.bfloat16)


def expert_chunk(xs, gs, wts, w, js, carried, last):
    length, width = xs[0].shape
    count = 2 * length
    n = len(js)
    half = w.shape[1] // (3 * n)
    tiles = count // TILE
    band = width // BANDS
    parts = 4 if last else 1
    sub = tiles // parts

    def early(size):
        return pl.BlockSpec((TILE, size), lambda i: (jnp.minimum(i, tiles - 1), 0))

    weight_sides = [
        pl.BlockSpec((EXP_DEV, TILE), lambda i, f=first: (0, jnp.clip(i - f, 0, tiles // 2 - 1)))
        for first in (0, tiles // 2)
    ]

    def late(part):
        return pl.BlockSpec(
            (TILE, width),
            lambda i: (jnp.clip(tiles - 1 - jnp.maximum(i - tiles, 0) - part * sub, 0, tiles // parts - 1), 0),
        )

    args = [*xs, *gs, *wts, w]
    specs = [
        *[pl.BlockSpec(memory_space=pl.ANY)] * 6,
        *weight_sides,
        pl.BlockSpec(w.shape, lambda i: (0, 0), pipeline_mode=pl.Buffered(1)),
    ]
    if carried is not None:
        args.append(carried)
        specs.append(
            pl.BlockSpec((TILE, width), lambda i: (tiles - 1 - jnp.maximum(i - tiles, 0), 0))
        )
    out = pl.pallas_call(
        functools.partial(expert_kernel, js[0], n, half, tiles, band, carried is not None, parts),
        grid=(2 * tiles,),
        in_specs=specs,
        out_specs=[
            *[late(part) for part in range(parts)],
            early(n * half),
            pl.BlockSpec((n, TILE), lambda i: (0, jnp.minimum(i, tiles - 1))),
            pl.BlockSpec((band, w.shape[1]), lambda i: (jnp.clip(i - tiles, 0, BANDS - 1), 0)),
        ],
        out_shape=[
            *[
                jax.ShapeDtypeStruct((count // parts, width), jnp.bfloat16 if last else jnp.float32)
                for _ in range(parts)
            ],
            jax.ShapeDtypeStruct((count, n * half), jnp.bfloat16),
            jax.ShapeDtypeStruct((n, count), jnp.float32),
            jax.ShapeDtypeStruct(w.shape, jnp.bfloat16),
        ],
        scratch_shapes=[
            pltpu.VMEM((count, width), jnp.bfloat16),
            pltpu.VMEM((count, width), jnp.bfloat16),
            pltpu.VMEM((count, n * half), jnp.bfloat16),
            pltpu.VMEM((count, 2 * n * half), jnp.bfloat16),
            pltpu.SemaphoreType.DMA((2, tiles)),
        ],
        compiler_params=pltpu.CompilerParams(vmem_limit_bytes=60 * 1024 * 1024),
        cost_estimate=pl.CostEstimate(
            flops=10 * count * n * half * width,
            bytes_accessed=8 * count * width + 4 * width * n * half * 3,
            transcendentals=count * n * half,
        ),
        name="experts",
    )(*args)
    return (out[:parts] if last else out[0]), *out[parts:]


def mix_kernel(n, parts, *refs):
    refs = refs[: 2 * n] + refs[2 * n + 1 :]
    total = dot(refs[0][...], refs[n][...], 1, 1)
    for i in range(1, n):
        total = total + dot(refs[i][...], refs[n + i][...], 1, 1)
    step, steps = pl.program_id(0), pl.num_programs(0)
    for part in range(parts):

        @pl.when((steps - 1 - step) * parts // steps == part)
        def _():
            refs[2 * n + part][...] = total.astype(jnp.bfloat16)


def mix_experts(scaled, weights, behind):
    count, width = scaled[0].shape[0], weights[0].shape[0]
    n, parts, steps = len(scaled), 4, count // TILE
    sub = steps // parts

    def late(part):
        return pl.BlockSpec((TILE, width), lambda i: (jnp.clip(steps - 1 - i - part * sub, 0, sub - 1), 0))

    return pl.pallas_call(
        functools.partial(mix_kernel, n, parts),
        grid=(steps,),
        in_specs=[pl.BlockSpec((TILE, s.shape[1]), lambda i: (steps - 1 - i, 0)) for s in scaled]
        + [pl.BlockSpec((width, s.shape[1]), lambda i: (0, 2)) for s in scaled]
        + [pl.BlockSpec(memory_space=pl.ANY)],
        out_specs=[late(part) for part in range(parts)],
        out_shape=[jax.ShapeDtypeStruct((count // parts, width), jnp.bfloat16) for _ in range(parts)],
        compiler_params=pltpu.CompilerParams(vmem_limit_bytes=60 * 1024 * 1024),
        cost_estimate=pl.CostEstimate(
            flops=2 * count * width * sum(s.shape[1] for s in scaled),
            bytes_accessed=4 * count * width,
            transcendentals=0,
        ),
        name="mix_experts",
    )(*scaled, *weights, behind)


def swap_member(v, bit):
    n = lax.axis_size("expert")
    return lax.ppermute(v, "expert", [(i, i ^ bit) for i in range(n)])


def swap_shard(v):
    n = lax.axis_size("shard")
    return lax.ppermute(v, "shard", [(i, i ^ 1) for i in range(n)])


def after(v, behind):
    return pl.pallas_call(
        lambda *refs: None,
        in_specs=[pl.BlockSpec(memory_space=pl.ANY)] * 2,
        out_specs=pl.BlockSpec(memory_space=pl.ANY),
        out_shape=jax.ShapeDtypeStruct(v.shape, v.dtype),
        input_output_aliases={0: 0},
        name="after",
    )(v, behind)


def swap_sequence(v):
    got = swap_shard(v[: v.shape[0] // 2])
    return [got, swap_member(got, 1)]


def chip_bits():
    n = lax.axis_size("expert")
    return [1 << i for i in range(1, n.bit_length() - 1)]


def gather_members(v, axis=0):
    for bit in chip_bits() + [1]:
        v = jnp.concatenate([v, swap_member(v, bit)], axis=axis)
    return v


def gather_heads(v):
    members = lax.axis_size("expert")
    width = v.shape[1] // members
    for bit in chip_bits() + [1]:
        got = swap_member(v, bit)
        source = [place_of(2 * (p % (members // 2)) + p // (members // 2), bit, members) for p in range(members)]
        got = jnp.concatenate([got[:, p * width : (p + 1) * width] for p in source], axis=1)
        v = jnp.concatenate([v, got], axis=0)
    return v


def halves(v, axis):
    return jnp.split(v, 2, axis=axis)


def add_swapped(keep, sent, swap):
    return keep.astype(jnp.float32) + swap(sent).astype(jnp.float32)


def scatter_chip(v, axis):
    for bit in reversed(chip_bits()):
        keep, sent = halves(v, axis)
        v = add_swapped(keep, sent, lambda u: swap_member(u, bit)).astype(v.dtype)
    return v


def scatter_members(parts, axis=0):
    kind = parts[0].dtype
    other = add_swapped(parts[2], parts[3], lambda u: swap_member(u, 1)).astype(kind)
    own = add_swapped(parts[0], parts[1], lambda u: swap_member(u, 1)).astype(kind)
    if axis == 1:
        return scatter_chip(add_swapped(own, other, swap_shard), axis)
    cut = own.shape[1] // 2
    one = scatter_chip(add_swapped(own[:, :cut], other[:, :cut], swap_shard).astype(kind), 0)
    two, two_other = scatter_chip(own[:, cut:], 0), scatter_chip(other[:, cut:], 0)
    two = add_swapped(two, two_other, swap_shard)
    return jnp.concatenate([one.astype(jnp.float32), two], axis=1)


def turn(first, back=False):
    members, shards = lax.axis_size("expert"), lax.axis_size("shard")
    pairs = []
    for e in range(members):
        for s in range(shards):
            core, low = e & 1, s & 1
            to_core, to_low = (low, core) if first else (1 - low, core)
            target = ((e & ~1) | to_core) * shards + ((s & ~1) | to_low)
            pairs.append((e * shards + s, target))
    if back:
        pairs = [(b, a) for a, b in pairs]
    return pairs


def permute_all(v, pairs):
    return lax.ppermute(v, ("expert", "shard"), pairs)


def shard_lines():
    n = lax.axis_size("shard")
    return [[s for s in range(n) if s & 1 == low] for low in range(2)]


def ring():
    n = lax.axis_size("shard")
    wide = n // 4
    walk = [(z, 0) for z in range(4)]
    for i, z in enumerate(reversed(range(4))):
        ys = range(1, wide)
        walk += [(z, y) for y in (ys if i % 2 == 0 else reversed(ys))]
    return [z * wide + y for z, y in walk]


def ring_step(v, by):
    walk = ring()
    n = len(walk)
    return lax.ppermute(v, "shard", [(walk[i], walk[(i + by) % n]) for i in range(n)])


def place_kernel(n, owner_ref, *refs):
    size = refs[0].shape[0]
    for i in range(n):
        refs[n][pl.ds(pl.multiple_of(owner_ref[i] * size, 16), size), :] = refs[i][...]


def ring_gather(v):
    n = lax.axis_size("shard")
    walk = ring()
    place = [walk.index(i) for i in range(n)]
    here = jnp.asarray(place, jnp.int32)[lax.axis_index("shard")]
    pieces, offsets = [v], [0]
    forth = back = v
    for k in range(1, n // 2 + 1):
        forth = ring_step(forth, 1)
        pieces.append(forth)
        offsets.append(-k)
        if k < n // 2:
            back = ring_step(back, -1)
            pieces.append(back)
            offsets.append(k)
    owners = jnp.asarray(walk, jnp.int32)[(here + jnp.asarray(offsets, jnp.int32)) % n]
    rows, size = v.shape
    return pl.pallas_call(
        functools.partial(place_kernel, n),
        grid_spec=pltpu.PrefetchScalarGridSpec(
            num_scalar_prefetch=1,
            grid=(1,),
            in_specs=[pl.BlockSpec((rows, size), lambda i, o: (0, 0))] * n,
            out_specs=pl.BlockSpec((rows * n, size), lambda i, o: (0, 0)),
        ),
        out_shape=jax.ShapeDtypeStruct((rows * n, size), v.dtype),
        compiler_params=pltpu.CompilerParams(vmem_limit_bytes=48 * 1024 * 1024),
        name="place",
    )(owners, *pieces)


def gather_shard(v):
    return lax.all_gather(v, "shard", axis=0, tiled=True)


def scatter_shard(v):
    return lax.psum_scatter(v, "shard", scatter_dimension=0, tiled=True)


def out_kernel(members, me_ref, slice_ref, out_ref):
    size = slice_ref.shape[2]
    p = pl.program_id(0)
    r = 2 * (p % (members // 2)) + p // (members // 2)
    col = pl.multiple_of((me_ref[0] ^ r) * size, 128)
    for a in range(members):
        row = pl.multiple_of(place_of(a, me_ref[0], members) * size, 16)
        out_ref[pl.ds(row, size), pl.ds(col, size)] = slice_ref[0, a * size : (a + 1) * size, :]


def assemble_out(me, slices):
    members, rows, size = slices.shape
    return pl.pallas_call(
        functools.partial(out_kernel, members),
        grid_spec=pltpu.PrefetchScalarGridSpec(
            num_scalar_prefetch=1,
            grid=(members,),
            in_specs=[pl.BlockSpec((1, rows, size), lambda p, me: (p, 0, 0))],
            out_specs=pl.BlockSpec((rows, size * members), lambda p, me: (0, 0)),
        ),
        out_shape=jax.ShapeDtypeStruct((rows, size * members), slices.dtype),
        compiler_params=pltpu.CompilerParams(vmem_limit_bytes=48 * 1024 * 1024),
        name="assemble_out",
    )(me, slices)


def body(
    tokens,
    segment_ids,
    routes,
    gain_attn,
    w_query,
    key_weight,
    value_weight,
    w_out,
    gain_ffn,
    w_router,
    w_gate_up,
    w_down,
    cotangent,
):
    bf16, f32 = jnp.bfloat16, jnp.float32
    members = lax.axis_size("expert")
    shards = lax.axis_size("shard")
    me = lax.axis_index("expert")
    core = me & 1
    low = lax.axis_index("shard") & 1
    rows, width = tokens.shape[1:]
    length = rows * members
    experts = EXP_DEV * members
    q_cols = QUERY_HEADS * HEAD_SIZE // members
    k_cols = KEY_VALUE_HEADS * HEAD_SIZE // members
    heads, kv_heads = q_cols // HEAD_SIZE, k_cols // HEAD_SIZE
    out_rows = width // (members * shards)
    half = FF // 2
    step = 2 if length <= 1024 else 1
    chunks = [tuple(range(i, min(i + step, EXP_DEV))) for i in range(0, EXP_DEV, step)]
    me_ref = me[None].astype(jnp.int32)

    def cols(w, n):
        return lax.dynamic_slice_in_dim(w, me * n, n, axis=1)

    small = jnp.concatenate([w_router, gain_attn[:, None], gain_ffn[:, None]], axis=1)
    total_cols = q_cols + 2 * k_cols
    first = jnp.concatenate(
        [
            cols(w_query, q_cols),
            cols(key_weight, k_cols),
            cols(value_weight, k_cols),
            jnp.pad(small, ((0, 0), (0, 128 - small.shape[1]))),
        ],
        axis=1,
    )
    first = gather_shard(first)
    full_qkv = first[:, :total_cols]
    full_small = first[:, total_cols:]
    full_router = full_small[:, :experts]
    gain_one = full_small[:, experts].astype(f32)
    gain_two = full_small[:, experts + 1].astype(f32)

    all_tokens = gather_members(tokens[0])
    meta = jnp.concatenate([segment_ids, routes[0].T], axis=0)
    meta = gather_members(meta, axis=1)
    seg = meta[0]
    my_routes = meta[1:]
    my_grad = gather_members(after(cotangent[0], all_tokens))
    all_grad = [my_grad, *swap_sequence(my_grad)]
    out_slice = ring_gather(after(cols(w_out, q_cols), all_tokens))

    weights = []
    for js in chunks:
        sides = [
            jnp.concatenate(
                [w_gate_up[:, j, h * half : (h + 1) * half] for j in js]
                + [w_gate_up[:, j, FF + h * half : FF + (h + 1) * half] for j in js]
                + [w_down[:, j, h * half : (h + 1) * half] for j in js],
                axis=1,
            )
            for h in range(2)
        ]
        one = permute_all(jnp.where(low == 0, sides[0], sides[1]), turn(True))
        two = permute_all(jnp.where(low == 0, sides[1], sides[0]), turn(False))
        block = jnp.concatenate(
            [jnp.where(core == 0, one, two), jnp.where(core == 0, two, one)], axis=0
        )
        weights.append(
            lax.all_gather(block, "shard", axis=0, tiled=True, axis_index_groups=shard_lines())
        )

    inputs = all_tokens.astype(f32)
    normed_one = inputs * inverse_rms(inputs)
    xn_one = (normed_one * gain_one).astype(bf16)
    qkv = dot(full_qkv, xn_one, 0, 1).reshape(heads + 2 * kv_heads, HEAD_SIZE, length)
    order = jnp.arange(members, dtype=jnp.int32)
    order = me ^ (2 * (order % (members // 2)) + order // (members // 2))
    positions = (order[:, None] * rows + jnp.arange(rows, dtype=jnp.int32)[None, :]).reshape(-1)
    cosine, sine = rope_tables(positions)
    rotated = rotate(qkv[: heads + kv_heads], cosine, sine).astype(bf16)
    queries = rotated[:heads] * jnp.asarray(HEAD_SIZE**-0.5, bf16)
    keys = rotated[heads:]
    values = qkv[heads + kv_heads :].astype(bf16)
    attended, lse = attention_forward(me_ref, queries, keys, values, seg)
    attended_rows = attended.reshape(q_cols, length)
    attended_all = gather_heads(attended_rows)
    full_out = assemble_out(me_ref, gather_members(out_slice[None]))

    hidden = inputs + dot(attended_all, full_out, 0, 0)
    normed_two = hidden * inverse_rms(hidden)
    my_xn_two = (normed_two * gain_two).astype(bf16)
    xn_two = [my_xn_two, *swap_sequence(my_xn_two)]

    logits = dot(full_router, my_xn_two, 0, 1)
    named = jnp.any(
        my_routes[:, None, :] == jnp.arange(experts, dtype=jnp.int32)[None, :, None], axis=0
    )
    peak = jnp.max(jnp.where(named, logits, -jnp.inf), axis=0, keepdims=True)
    exps = jnp.where(named, jnp.exp(jnp.minimum(logits - peak, 0.0)), 0.0)
    gates = exps / jnp.sum(exps, axis=0, keepdims=True)
    group = (me & ~1) | low
    my_gates = [
        lax.dynamic_slice_in_dim(v, group * EXP_DEV, EXP_DEV, axis=0)
        for v in (gates, swap_shard(gates))
    ]

    count = 2 * length
    grad_in = None
    gate_grads, expert_grads, scaled = [], [], []
    for js, w in zip(chunks, weights):
        grad_in, s, gg, grads = expert_chunk(
            xn_two, all_grad, my_gates, w, js, grad_in, js is chunks[-1]
        )
        scaled.append(s)
        gate_grads.append(gg)
        expert_grads.append(
            lax.psum_scatter(
                grads, "shard", scatter_dimension=0, tiled=True, axis_index_groups=shard_lines()
            )
        )

    grad_xn_two = scatter_members(grad_in)
    gate_grads = jnp.tile(jnp.concatenate(gate_grads, axis=0), (members, 1))
    mine = jnp.arange(experts, dtype=jnp.int32)[:, None] // EXP_DEV == group
    gate_grads = jnp.where(mine, gate_grads, 0.0)
    grad_gates = scatter_members(jnp.split(gate_grads, 4, axis=1), axis=1)
    own_gates = gates[:, :rows]
    grad_chosen = own_gates * (grad_gates - jnp.sum(own_gates * grad_gates, axis=0, keepdims=True))
    grad_logits = grad_chosen.astype(bf16)
    grad_xn_two = grad_xn_two + dot(grad_logits, full_router, 0, 1)
    my_hidden = hidden[:rows]

    my_scale = inverse_rms(my_hidden)
    my_normed = my_hidden * my_scale
    grad_gain_two = jnp.sum(grad_xn_two * my_normed, axis=0)
    g = grad_xn_two * gain_two
    grad_hidden = cotangent[0].astype(f32) + my_scale * (
        g - my_normed * jnp.mean(g * my_normed, axis=-1, keepdims=True)
    )
    grad_attn = gather_members(grad_hidden.astype(bf16))
    grad_attended = dot(full_out[:q_cols], grad_attn, 1, 1).astype(bf16)
    grad_attended = grad_attended.reshape(heads, HEAD_SIZE, length)
    grad_out = jnp.dot(attended_rows, grad_attn, preferred_element_type=f32)
    grad_router = dot(my_xn_two[:rows], grad_logits, 0, 1)

    dq, dk, dv = attention_backward(me_ref, queries, keys, values, attended, grad_attended, lse, seg)
    dq = rotate(dq, cosine, -sine) * HEAD_SIZE**-0.5
    dk = rotate(dk, cosine, -sine)
    grad_qkv = jnp.concatenate([dq, dk, dv], axis=0).astype(bf16).reshape(-1, length)
    grad_first = dot(xn_one, grad_qkv, 0, 1)
    grad_xn_one = dot(grad_qkv, full_qkv, 0, 1)
    grad_gain_one = jnp.sum(grad_xn_one * normed_one, axis=0)
    grad_xn_one = grad_xn_one.astype(bf16)
    for bit in [1] + chip_bits()[::-1]:
        keep, sent = halves(grad_xn_one.astype(bf16), 0)
        grad_xn_one = add_swapped(keep, sent, lambda u: swap_member(u, bit))
    my_inputs = tokens[0].astype(f32)
    scale_one = inverse_rms(my_inputs)
    normed = my_inputs * scale_one
    h = grad_xn_one * gain_one
    grad_tokens = grad_hidden + scale_one * (h - normed * jnp.mean(h * normed, axis=-1, keepdims=True))

    rest = jnp.concatenate([grad_router, grad_gain_one[:, None], grad_gain_two[:, None]], axis=1)
    rest = jnp.pad(rest, ((0, 0), (0, 128 - rest.shape[1])))
    grad_first = jnp.concatenate([grad_first, rest], axis=1).astype(bf16)
    grad_first = jnp.transpose(grad_first.reshape(members, shards, out_rows, -1), (1, 0, 2, 3))
    grad_out = jnp.transpose(
        grad_out.astype(bf16).reshape(shards, out_rows, members, q_cols), (0, 2, 1, 3)
    )
    grad_first = jnp.concatenate([grad_first, grad_out], axis=3)
    grad_first = scatter_shard(grad_first.reshape(width, -1)).reshape(members, out_rows, -1)
    out_grads = jnp.transpose(grad_first[:, :, total_cols + 128 :], (1, 0, 2)).astype(f32)
    grad_first = grad_first[:, :, : total_cols + 128]
    grad_first = lax.all_to_all(grad_first, "expert", split_axis=0, concat_axis=0, tiled=True)
    rest = jnp.sum(grad_first[:, :, total_cols:].astype(f32), axis=0)
    grad_first = jnp.transpose(grad_first, (1, 0, 2)).astype(f32)

    mixed = my_hidden + scatter_members(mix_experts(scaled, weights, grad_attn))

    gate_up_out, down_out = [], []
    one = None
    for js, v in zip(chunks, expert_grads):
        if one is not None:
            v, one = lax.optimization_barrier((v, one))
        size = v.shape[0] // 2
        one = permute_all(jnp.where(core == 0, v[:size], v[size:]), turn(True, True))
        two = permute_all(jnp.where(core == 0, v[size:], v[:size]), turn(False, True))
        sides = [jnp.where(low == 0, one, two), jnp.where(low == 0, two, one)]
        n = len(js)
        for i in range(n):
            piece = [
                [sides[h][:, (k * n + i) * half : (k * n + i + 1) * half] for h in range(2)]
                for k in range(3)
            ]
            gate_up_out.append(jnp.concatenate(piece[0] + piece[1], axis=1))
            down_out.append(jnp.concatenate(piece[2], axis=1))
    return (
        mixed.astype(bf16)[None],
        grad_tokens.astype(bf16)[None],
        rest[:, experts],
        grad_first[:, :, :q_cols].reshape(out_rows, -1),
        grad_first[:, :, q_cols : q_cols + k_cols].reshape(out_rows, -1),
        grad_first[:, :, q_cols + k_cols : total_cols].reshape(out_rows, -1),
        out_grads.reshape(out_rows, -1),
        rest[:, experts + 1],
        rest[:, :experts],
        jnp.stack(gate_up_out, axis=1).astype(f32),
        jnp.stack(down_out, axis=1).astype(f32),
    )


def solution(mesh):
    in_specs = (
        P("shard", "expert", None),
        P("shard", "expert"),
        P("shard", "expert", None),
        P("shard"),
        P("shard", None),
        P("shard", None),
        P("shard", None),
        P("shard", None),
        P("shard"),
        P("shard", None),
        P("shard", "expert", None),
        P("shard", "expert", None),
        P("shard", "expert", None),
    )
    out_specs = (
        P("shard", "expert", None),
        P("shard", "expert", None),
        P(("expert", "shard")),
        P(("expert", "shard"), None),
        P(("expert", "shard"), None),
        P(("expert", "shard"), None),
        P(("expert", "shard"), None),
        P(("expert", "shard")),
        P(("expert", "shard"), None),
        P("shard", "expert", None),
        P("shard", "expert", None),
    )
    return jax.shard_map(body, mesh=mesh, in_specs=in_specs, out_specs=out_specs, check_vma=False)
```

```python
import functools

import jax
import jax.numpy as jnp
from jax import lax
from jax.experimental import pallas as pl
from jax.experimental.pallas import tpu as pltpu
from jax.sharding import PartitionSpec as P

QUERY_HEADS = 24
KEY_VALUE_HEADS = 8
GROUP = QUERY_HEADS // KEY_VALUE_HEADS
HEAD_SIZE = 64
HALF = HEAD_SIZE // 2
FF = 512
TOP = 8
EXP_DEV = 5
BLOCK = 256
TILE = 512
BANDS = 4
MASKED = -1e30
epsilon = 1e-06


def dot(a, b, ca, cb):
    return lax.dot_general(a, b, (((ca,), (cb,)), ((), ())), preferred_element_type=jnp.float32)


def inverse_rms(v):
    return lax.rsqrt(jnp.mean(v * v, axis=-1, keepdims=True) + epsilon)


def place_of(block, mine, members):
    r = block ^ mine
    return (r & 1) * (members // 2) + (r >> 1)


def spans(me_ref, blocks):
    return [pl.multiple_of(place_of(a, me_ref[0], blocks) * BLOCK, BLOCK) for a in range(blocks)]


def allowed_tile(seg_col, seg_row, at, qi, ki):
    ok = seg_col[pl.ds(at[ki], BLOCK), :] == seg_row[:, pl.ds(at[qi], BLOCK)]
    if qi == ki:
        kpos = lax.broadcasted_iota(jnp.int32, (BLOCK, BLOCK), 0)
        qpos = lax.broadcasted_iota(jnp.int32, (BLOCK, BLOCK), 1)
        ok = ok & (kpos <= qpos)
    return ok


def attention_forward_kernel(blocks, me_ref, q_ref, k_ref, v_ref, seg_col, seg_row, o_ref, lse_ref, keys):
    at = spans(me_ref, blocks)
    keys[...] = k_ref[0].astype(jnp.float32).T.astype(jnp.bfloat16)
    for qi in range(blocks):
        qs = pl.ds(at[qi], BLOCK)
        q = q_ref[0, :, qs]
        top = total = acc = None
        for ki in range(qi, -1, -1):
            ks = pl.ds(at[ki], BLOCK)
            s = dot(keys[ks, :], q, 1, 0)
            s = jnp.where(allowed_tile(seg_col, seg_row, at, qi, ki), s, MASKED)
            peak = jnp.max(s, axis=0, keepdims=True)
            if top is None:
                top = peak
                e = jnp.exp(s - top)
                total = jnp.sum(e, axis=0, keepdims=True)
                acc = dot(v_ref[0, :, ks], e.astype(jnp.bfloat16), 1, 0)
            else:
                new = jnp.maximum(top, peak)
                scale = jnp.exp(top - new)
                e = jnp.exp(s - new)
                total = total * scale + jnp.sum(e, axis=0, keepdims=True)
                acc = acc * scale + dot(v_ref[0, :, ks], e.astype(jnp.bfloat16), 1, 0)
                top = new
        o_ref[0, :, qs] = (acc / total).astype(jnp.bfloat16)
        lse_ref[0, :, qs] = top + jnp.log(total)


def attention_forward(me, q, k, v, seg):
    heads, _, length = q.shape
    blocks = length // BLOCK
    full = pl.BlockSpec((1, HEAD_SIZE, length), lambda h, me: (h, 0, 0))
    shared = pl.BlockSpec((1, HEAD_SIZE, length), lambda h, me: (h // GROUP, 0, 0))
    return pl.pallas_call(
        functools.partial(attention_forward_kernel, blocks),
        grid_spec=pltpu.PrefetchScalarGridSpec(
            num_scalar_prefetch=1,
            grid=(heads,),
            in_specs=[
                full,
                shared,
                shared,
                pl.BlockSpec((length, 1), lambda h, me: (0, 0)),
                pl.BlockSpec((1, length), lambda h, me: (0, 0)),
            ],
            out_specs=[full, pl.BlockSpec((1, 1, length), lambda h, me: (h, 0, 0))],
            scratch_shapes=[pltpu.VMEM((length, HEAD_SIZE), jnp.bfloat16)],
        ),
        out_shape=[
            jax.ShapeDtypeStruct((heads, HEAD_SIZE, length), jnp.bfloat16),
            jax.ShapeDtypeStruct((heads, 1, length), jnp.float32),
        ],
        compiler_params=pltpu.CompilerParams(vmem_limit_bytes=48 * 1024 * 1024),
        cost_estimate=pl.CostEstimate(
            flops=50 * heads * length * length * HEAD_SIZE,
            bytes_accessed=6 * heads * length * HEAD_SIZE,
            transcendentals=heads * length * length // 2,
        ),
        name="attention_forward",
    )(me, q, k, v, seg[:, None], seg[None, :])


def attention_backward_kernel(
    blocks, me_ref, q_ref, k_ref, v_ref, o_ref, g_ref, lse_ref, seg_col, seg_row,
    dq_ref, dk_ref, dv_ref, keys, values, dk_acc, dv_acc,
):
    at = spans(me_ref, blocks)
    member = pl.program_id(1)

    @pl.when(member == 0)
    def _():
        dk_acc[...] = jnp.zeros_like(dk_acc)
        dv_acc[...] = jnp.zeros_like(dv_acc)
        keys[...] = k_ref[0].astype(jnp.float32).T.astype(jnp.bfloat16)
        values[...] = v_ref[0].astype(jnp.float32).T.astype(jnp.bfloat16)

    for qi in range(blocks):
        qs = pl.ds(at[qi], BLOCK)
        q = q_ref[0, :, qs]
        g = g_ref[0, :, qs]
        g32 = g.astype(jnp.float32)
        delta = jnp.sum(g32 * o_ref[0, :, qs].astype(jnp.float32), axis=0, keepdims=True)
        lse = lse_ref[0, :, qs]
        q_rows = q.astype(jnp.float32).T.astype(jnp.bfloat16)
        g_rows = g32.T.astype(jnp.bfloat16)
        dq = jnp.zeros((HEAD_SIZE, BLOCK), jnp.float32)
        for ki in range(qi + 1):
            ks = pl.ds(at[ki], BLOCK)
            s = dot(keys[ks, :], q, 1, 0)
            p = jnp.where(allowed_tile(seg_col, seg_row, at, qi, ki), jnp.exp(s - lse), 0.0)
            dp = dot(values[ks, :], g, 1, 0)
            ds = (p * (dp - delta)).astype(jnp.bfloat16)
            dv_acc[ks, :] += dot(p.astype(jnp.bfloat16), g_rows, 1, 0)
            dk_acc[ks, :] += dot(ds, q_rows, 1, 0)
            dq = dq + dot(k_ref[0, :, ks], ds, 1, 0)
        dq_ref[0, :, qs] = dq

    @pl.when(member == GROUP - 1)
    def _():
        dk_ref[0] = dk_acc[...].T
        dv_ref[0] = dv_acc[...].T


def attention_backward(me, q, k, v, o, g, lse, seg):
    heads, _, length = q.shape
    blocks = length // BLOCK
    full = pl.BlockSpec((1, HEAD_SIZE, length), lambda j, m, me: (j * GROUP + m, 0, 0))
    shared = pl.BlockSpec((1, HEAD_SIZE, length), lambda j, m, me: (j, 0, 0))
    return pl.pallas_call(
        functools.partial(attention_backward_kernel, blocks),
        grid_spec=pltpu.PrefetchScalarGridSpec(
            num_scalar_prefetch=1,
            grid=(heads // GROUP, GROUP),
            in_specs=[
                full,
                shared,
                shared,
                full,
                full,
                pl.BlockSpec((1, 1, length), lambda j, m, me: (j * GROUP + m, 0, 0)),
                pl.BlockSpec((length, 1), lambda j, m, me: (0, 0)),
                pl.BlockSpec((1, length), lambda j, m, me: (0, 0)),
            ],
            out_specs=[full, shared, shared],
            scratch_shapes=[
                pltpu.VMEM((length, HEAD_SIZE), jnp.bfloat16),
                pltpu.VMEM((length, HEAD_SIZE), jnp.bfloat16),
                pltpu.VMEM((length, HEAD_SIZE), jnp.float32),
                pltpu.VMEM((length, HEAD_SIZE), jnp.float32),
            ],
        ),
        out_shape=[
            jax.ShapeDtypeStruct((heads, HEAD_SIZE, length), jnp.float32),
            jax.ShapeDtypeStruct((heads // GROUP, HEAD_SIZE, length), jnp.float32),
            jax.ShapeDtypeStruct((heads // GROUP, HEAD_SIZE, length), jnp.float32),
        ],
        compiler_params=pltpu.CompilerParams(vmem_limit_bytes=48 * 1024 * 1024),
        cost_estimate=pl.CostEstimate(
            flops=46 * heads * length * length * HEAD_SIZE,
            bytes_accessed=16 * heads * length * HEAD_SIZE,
            transcendentals=heads * length * length // 2,
        ),
        name="attention_backward",
    )(me, q, k, v, o, g, lse, seg[:, None], seg[None, :])


def rope_tables(positions):
    freqs = 10000.0 ** (-(jnp.arange(HALF, dtype=jnp.float32) * 2.0 / HEAD_SIZE))
    angles = freqs[:, None] * positions.astype(jnp.float32)[None, :]
    return jnp.cos(angles)[None], jnp.sin(angles)[None]


def rotate(v, cosine, sine):
    a, b = v[:, :HALF, :], v[:, HALF:, :]
    return jnp.concatenate([a * cosine - b * sine, b * cosine + a * sine], axis=1)


def side_tiles(tiles):
    return [(0, tiles // 2), (tiles // 2, tiles // 4), (3 * tiles // 4, tiles // 4)]


def expert_kernel(start, n, half, tiles, band, has_in, parts, *refs):
    refs = list(refs)
    x_refs = refs[:3]
    g_refs = refs[3:6]
    wt_refs = refs[6:8]
    w_ref = refs[8]
    refs = refs[9:]
    gin_in = refs.pop(0) if has_in else None
    gin_refs, refs = refs[:parts], refs[parts:]
    s_ref, gg_ref, dw_ref, xs, gs, ss, bs, sems = refs
    step = pl.program_id(0)
    later = step - tiles
    m = 2 * n * half
    arrivals = []
    for side, (first, size) in enumerate(side_tiles(tiles)):
        for i in range(size):
            to = slice((first + i) * TILE, (first + i + 1) * TILE)
            arrivals.append(
                [
                    pltpu.make_async_copy(
                        sources[side].at[slice(i * TILE, (i + 1) * TILE), :],
                        target.at[to, :],
                        sems.at[k, first + i],
                    )
                    for k, (sources, target) in enumerate(((x_refs, xs), (g_refs, gs)))
                ]
            )

    @pl.when(step == 0)
    def _():
        for pair in arrivals:
            for copy in pair:
                copy.start()

    for i, pair in enumerate(arrivals):

        @pl.when(step == i)
        def _():
            for copy in pair:
                copy.wait()

    @pl.when(step < tiles)
    def _():
        at = pl.ds(pl.multiple_of(step * TILE, TILE), TILE)
        x = xs[at, :]
        g = gs[at, :]
        weights = jnp.where(step < tiles // 2, wt_refs[0][...], wt_refs[1][...]).T
        sums = []
        for i in range(n):
            c = [slice((k * n + i) * half, (k * n + i + 1) * half) for k in range(3)]
            gate = dot(x, w_ref[:, c[0]], 1, 0)
            up = dot(x, w_ref[:, c[1]], 1, 0)
            through = dot(g, w_ref[:, c[2]], 1, 0)
            weight = weights[:, start + i : start + i + 1]
            sig = jax.nn.sigmoid(gate)
            soft = gate * sig
            act = soft * up
            sums.append(jnp.sum(act * through, axis=1, keepdims=True))
            scaled = (weight * act).astype(jnp.bfloat16)
            ss[at, c[0]] = scaled
            s_ref[:, c[0]] = scaled
            grad = weight * through
            bs[at, c[0]] = (grad * up * sig * (1.0 + gate * (1.0 - sig))).astype(jnp.bfloat16)
            bs[at, c[1]] = (grad * soft).astype(jnp.bfloat16)
        gg_ref[...] = jnp.concatenate(sums, axis=1).T

    @pl.when(later >= 0)
    def _():
        tile = tiles - 1 - later
        at = pl.ds(pl.multiple_of(tile * TILE, TILE), TILE)
        gin = dot(bs[at, :], w_ref[:, :m], 1, 1)
        if has_in:
            gin = gin + gin_in[...]
        if parts == 1:
            gin_refs[0][...] = gin
        else:
            for part in range(parts):

                @pl.when(tile * parts // tiles == part)
                def _():
                    gin_refs[part][...] = gin.astype(jnp.bfloat16)

    @pl.when((later >= 0) & (later < BANDS))
    def _():
        at = pl.ds(pl.multiple_of(later * band, band), band)
        dw_ref[:, :m] = dot(xs[:, at], bs[...], 0, 0).astype(jnp.bfloat16)
        dw_ref[:, m:] = dot(gs[:, at], ss[...], 0, 0).astype(jnp.bfloat16)


def expert_chunk(xs, gs, wts, w, js, carried, last):
    length, width = xs[0].shape
    count = 2 * length
    n = len(js)
    half = w.shape[1] // (3 * n)
    tiles = count // TILE
    band = width // BANDS
    parts = 4 if last else 1
    sub = tiles // parts

    def early(size):
        return pl.BlockSpec((TILE, size), lambda i: (jnp.minimum(i, tiles - 1), 0))

    weight_sides = [
        pl.BlockSpec((EXP_DEV, TILE), lambda i, f=first: (0, jnp.clip(i - f, 0, tiles // 2 - 1)))
        for first in (0, tiles // 2)
    ]

    def late(part):
        return pl.BlockSpec(
            (TILE, width),
            lambda i: (jnp.clip(tiles - 1 - jnp.maximum(i - tiles, 0) - part * sub, 0, tiles // parts - 1), 0),
        )

    args = [*xs, *gs, *wts, w]
    specs = [
        *[pl.BlockSpec(memory_space=pl.ANY)] * 6,
        *weight_sides,
        pl.BlockSpec(w.shape, lambda i: (0, 0), pipeline_mode=pl.Buffered(1)),
    ]
    if carried is not None:
        args.append(carried)
        specs.append(
            pl.BlockSpec((TILE, width), lambda i: (tiles - 1 - jnp.maximum(i - tiles, 0), 0))
        )
    out = pl.pallas_call(
        functools.partial(expert_kernel, js[0], n, half, tiles, band, carried is not None, parts),
        grid=(2 * tiles,),
        in_specs=specs,
        out_specs=[
            *[late(part) for part in range(parts)],
            early(n * half),
            pl.BlockSpec((n, TILE), lambda i: (0, jnp.minimum(i, tiles - 1))),
            pl.BlockSpec((band, w.shape[1]), lambda i: (jnp.clip(i - tiles, 0, BANDS - 1), 0)),
        ],
        out_shape=[
            *[
                jax.ShapeDtypeStruct((count // parts, width), jnp.bfloat16 if last else jnp.float32)
                for _ in range(parts)
            ],
            jax.ShapeDtypeStruct((count, n * half), jnp.bfloat16),
            jax.ShapeDtypeStruct((n, count), jnp.float32),
            jax.ShapeDtypeStruct(w.shape, jnp.bfloat16),
        ],
        scratch_shapes=[
            pltpu.VMEM((count, width), jnp.bfloat16),
            pltpu.VMEM((count, width), jnp.bfloat16),
            pltpu.VMEM((count, n * half), jnp.bfloat16),
            pltpu.VMEM((count, 2 * n * half), jnp.bfloat16),
            pltpu.SemaphoreType.DMA((2, tiles)),
        ],
        compiler_params=pltpu.CompilerParams(vmem_limit_bytes=60 * 1024 * 1024),
        cost_estimate=pl.CostEstimate(
            flops=26 * count * n * half * width,
            bytes_accessed=8 * count * width + 4 * width * n * half * 3,
            transcendentals=count * n * half,
        ),
        name="experts",
    )(*args)
    return (out[:parts] if last else out[0]), *out[parts:]


def mix_kernel(n, parts, *refs):
    refs = refs[: 2 * n] + refs[2 * n + 1 :]
    total = dot(refs[0][...], refs[n][...], 1, 1)
    for i in range(1, n):
        total = total + dot(refs[i][...], refs[n + i][...], 1, 1)
    step, steps = pl.program_id(0), pl.num_programs(0)
    for part in range(parts):

        @pl.when((steps - 1 - step) * parts // steps == part)
        def _():
            refs[2 * n + part][...] = total.astype(jnp.bfloat16)


def mix_experts(scaled, weights, behind):
    count, width = scaled[0].shape[0], weights[0].shape[0]
    n, parts, steps = len(scaled), 4, count // TILE
    sub = steps // parts

    def late(part):
        return pl.BlockSpec((TILE, width), lambda i: (jnp.clip(steps - 1 - i - part * sub, 0, sub - 1), 0))

    return pl.pallas_call(
        functools.partial(mix_kernel, n, parts),
        grid=(steps,),
        in_specs=[pl.BlockSpec((TILE, s.shape[1]), lambda i: (steps - 1 - i, 0)) for s in scaled]
        + [pl.BlockSpec((width, s.shape[1]), lambda i: (0, 2)) for s in scaled]
        + [pl.BlockSpec(memory_space=pl.ANY)],
        out_specs=[late(part) for part in range(parts)],
        out_shape=[jax.ShapeDtypeStruct((count // parts, width), jnp.bfloat16) for _ in range(parts)],
        compiler_params=pltpu.CompilerParams(vmem_limit_bytes=60 * 1024 * 1024),
        cost_estimate=pl.CostEstimate(
            flops=4 * count * width * sum(s.shape[1] for s in scaled),
            bytes_accessed=4 * count * width,
            transcendentals=0,
        ),
        name="mix_experts",
    )(*scaled, *weights, behind)


def swap_member(v, bit):
    n = lax.axis_size("expert")
    return lax.ppermute(v, "expert", [(i, i ^ bit) for i in range(n)])


def swap_shard(v):
    n = lax.axis_size("shard")
    return lax.ppermute(v, "shard", [(i, i ^ 1) for i in range(n)])


def after(v, behind):
    return pl.pallas_call(
        lambda *refs: None,
        in_specs=[pl.BlockSpec(memory_space=pl.ANY)] * 2,
        out_specs=pl.BlockSpec(memory_space=pl.ANY),
        out_shape=jax.ShapeDtypeStruct(v.shape, v.dtype),
        input_output_aliases={0: 0},
        cost_estimate=pl.CostEstimate(flops=0, bytes_accessed=1024, transcendentals=0),
        name="after",
    )(v, behind)


def swap_sequence(v):
    got = swap_shard(v[: v.shape[0] // 2])
    return [got, swap_member(got, 1)]


def chip_bits():
    n = lax.axis_size("expert")
    return [1 << i for i in range(1, n.bit_length() - 1)]


def gather_members(v, axis=0):
    for bit in chip_bits() + [1]:
        v = jnp.concatenate([v, swap_member(v, bit)], axis=axis)
    return v


def gather_heads(v, *behind):
    members = lax.axis_size("expert")
    width = v.shape[1] // members
    for bit in chip_bits() + [1]:
        if bit == 1:
            for other in behind:
                v = after(v, other)
        got = swap_member(v, bit)
        source = [place_of(2 * (p % (members // 2)) + p // (members // 2), bit, members) for p in range(members)]
        got = jnp.concatenate([got[:, p * width : (p + 1) * width] for p in source], axis=1)
        v = jnp.concatenate([v, got], axis=0)
    return v


def halves(v, axis):
    return jnp.split(v, 2, axis=axis)


def add_swapped(keep, sent, swap):
    return keep.astype(jnp.float32) + swap(sent).astype(jnp.float32)


def scatter_chip(v, axis):
    for bit in reversed(chip_bits()):
        keep, sent = halves(v, axis)
        v = add_swapped(keep, sent, lambda u: swap_member(u, bit)).astype(v.dtype)
    return v


def scatter_members(parts, axis=0):
    kind = parts[0].dtype
    other = add_swapped(parts[2], parts[3], lambda u: swap_member(u, 1)).astype(kind)
    own = add_swapped(parts[0], parts[1], lambda u: swap_member(u, 1)).astype(kind)
    if axis == 1:
        return scatter_chip(add_swapped(own, other, swap_shard), axis)
    cut = own.shape[1] // 2
    one = add_swapped(own[:, :cut], other[:, :cut], swap_shard).astype(kind)
    halfway = one
    one = scatter_chip(one, 0)
    two, two_other = scatter_chip(own[:, cut:], 0), scatter_chip(other[:, cut:], 0)
    two = add_swapped(two, two_other, swap_shard)
    return jnp.concatenate([one.astype(jnp.float32), two], axis=1), halfway


def turn(first, back=False):
    members, shards = lax.axis_size("expert"), lax.axis_size("shard")
    pairs = []
    for e in range(members):
        for s in range(shards):
            core, low = e & 1, s & 1
            to_core, to_low = (low, core) if first else (1 - low, core)
            target = ((e & ~1) | to_core) * shards + ((s & ~1) | to_low)
            pairs.append((e * shards + s, target))
    if back:
        pairs = [(b, a) for a, b in pairs]
    return pairs


def permute_all(v, pairs):
    return lax.ppermute(v, ("expert", "shard"), pairs)


def shard_lines():
    n = lax.axis_size("shard")
    return [[s for s in range(n) if s & 1 == low] for low in range(2)]


def gather_line(v):
    return lax.all_gather(v, "shard", axis=0, tiled=True, axis_index_groups=shard_lines())


def scatter_line(v):
    return lax.psum_scatter(
        v, "shard", scatter_dimension=0, tiled=True, axis_index_groups=shard_lines()
    )


def merge_lines(v, low):
    n = lax.axis_size("shard") // 2
    got = swap_shard(v)
    v, got = v.reshape(n, -1, v.shape[1]), got.reshape(n, -1, v.shape[1])
    sides = [jnp.where(low == 0, v, got), jnp.where(low == 0, got, v)]
    return jnp.stack(sides, axis=1).reshape(-1, v.shape[2])


def split_lines(v, low):
    n = lax.axis_size("shard") // 2
    v = v.reshape(n, 2, -1, v.shape[1])
    keep, sent = jnp.where(low == 0, v[:, 0], v[:, 1]), jnp.where(low == 0, v[:, 1], v[:, 0])
    keep, sent = keep.reshape(-1, v.shape[3]), sent.reshape(-1, v.shape[3])
    return add_swapped(keep, sent, swap_shard).astype(v.dtype)


def out_kernel(members, me_ref, slice_ref, out_ref):
    size = slice_ref.shape[2]
    p = pl.program_id(0)
    r = 2 * (p % (members // 2)) + p // (members // 2)
    col = pl.multiple_of((me_ref[0] ^ r) * size, 128)
    for a in range(members):
        row = pl.multiple_of(place_of(a, me_ref[0], members) * size, 16)
        out_ref[pl.ds(row, size), pl.ds(col, size)] = slice_ref[0, a * size : (a + 1) * size, :]


def assemble_out(me, slices):
    members, rows, size = slices.shape
    return pl.pallas_call(
        functools.partial(out_kernel, members),
        grid_spec=pltpu.PrefetchScalarGridSpec(
            num_scalar_prefetch=1,
            grid=(members,),
            in_specs=[pl.BlockSpec((1, rows, size), lambda p, me: (p, 0, 0))],
            out_specs=pl.BlockSpec((rows, size * members), lambda p, me: (0, 0)),
        ),
        out_shape=jax.ShapeDtypeStruct((rows, size * members), slices.dtype),
        compiler_params=pltpu.CompilerParams(vmem_limit_bytes=48 * 1024 * 1024),
        cost_estimate=pl.CostEstimate(
            flops=0, bytes_accessed=4 * rows * size * members, transcendentals=0
        ),
        name="assemble_out",
    )(me, slices)


def body(
    tokens,
    segment_ids,
    routes,
    gain_attn,
    w_query,
    key_weight,
    value_weight,
    w_out,
    gain_ffn,
    w_router,
    w_gate_up,
    w_down,
    cotangent,
):
    bf16, f32 = jnp.bfloat16, jnp.float32
    members = lax.axis_size("expert")
    shards = lax.axis_size("shard")
    me = lax.axis_index("expert")
    core = me & 1
    low = lax.axis_index("shard") & 1
    rows, width = tokens.shape[1:]
    length = rows * members
    experts = EXP_DEV * members
    q_cols = QUERY_HEADS * HEAD_SIZE // members
    k_cols = KEY_VALUE_HEADS * HEAD_SIZE // members
    heads, kv_heads = q_cols // HEAD_SIZE, k_cols // HEAD_SIZE
    out_rows = width // (members * shards)
    half = FF // 2
    cuts = [0, 2, EXP_DEV] if length <= 1024 else range(EXP_DEV + 1)
    chunks = [tuple(range(a, b)) for a, b in zip(cuts[:-1], cuts[1:])]
    me_ref = me[None].astype(jnp.int32)

    def cols(w, n):
        return lax.dynamic_slice_in_dim(w, me * n, n, axis=1)

    all_tokens = gather_members(tokens[0])
    meta = jnp.concatenate([segment_ids, routes[0].T], axis=0)
    meta = gather_members(meta, axis=1)
    seg = meta[0]
    my_routes = meta[1:]
    my_grad = after(cotangent[0], all_tokens)
    for bit in chip_bits():
        my_grad = jnp.concatenate([my_grad, swap_member(my_grad, bit)], axis=0)
    grad_pair = my_grad
    my_grad = jnp.concatenate([my_grad, swap_member(my_grad, 1)], axis=0)

    small = jnp.concatenate([w_router, gain_attn[:, None], gain_ffn[:, None]], axis=1)
    total_cols = q_cols + 2 * k_cols
    first = jnp.concatenate(
        [
            cols(w_out, q_cols),
            cols(w_query, q_cols),
            cols(key_weight, k_cols),
            cols(value_weight, k_cols),
            jnp.pad(small, ((0, 0), (0, 128 - small.shape[1]))),
        ],
        axis=1,
    )
    first = gather_line(first)
    out_slice = first[:, :q_cols]
    first = merge_lines(after(first[:, q_cols:], grad_pair), low)
    out_slice = merge_lines(after(out_slice, first), low)
    full_qkv = first[:, :total_cols]
    full_small = first[:, total_cols:]
    full_router = full_small[:, :experts]
    gain_one = full_small[:, experts].astype(f32)
    gain_two = full_small[:, experts + 1].astype(f32)

    weights, blocks = [], []
    for js in chunks:
        sides = [
            jnp.concatenate(
                [w_gate_up[:, j, h * half : (h + 1) * half] for j in js]
                + [w_gate_up[:, j, FF + h * half : FF + (h + 1) * half] for j in js]
                + [w_down[:, j, h * half : (h + 1) * half] for j in js],
                axis=1,
            )
            for h in range(2)
        ]
        one = jnp.where(low == 0, sides[0], sides[1])
        two = jnp.where(low == 0, sides[1], sides[0])
        if blocks:
            one, two = after(one, out_slice), after(two, out_slice)
        one, two = permute_all(one, turn(True)), permute_all(two, turn(False))
        block = jnp.concatenate(
            [jnp.where(core == 0, one, two), jnp.where(core == 0, two, one)], axis=0
        )
        blocks.append(block)
        weights.append(
            gather_line(block)
        )

    inputs = all_tokens.astype(f32)
    normed_one = inputs * inverse_rms(inputs)
    xn_one = (normed_one * gain_one).astype(bf16)
    qkv = dot(full_qkv, xn_one, 0, 1).reshape(heads + 2 * kv_heads, HEAD_SIZE, length)
    order = jnp.arange(members, dtype=jnp.int32)
    order = me ^ (2 * (order % (members // 2)) + order // (members // 2))
    positions = (order[:, None] * rows + jnp.arange(rows, dtype=jnp.int32)[None, :]).reshape(-1)
    cosine, sine = rope_tables(positions)
    rotated = rotate(qkv[: heads + kv_heads], cosine, sine).astype(bf16)
    queries = rotated[:heads] * jnp.asarray(HEAD_SIZE**-0.5, bf16)
    keys = rotated[heads:]
    values = qkv[heads + kv_heads :].astype(bf16)
    attended, lse = attention_forward(me_ref, queries, keys, values, seg)
    attended_rows = attended.reshape(q_cols, length)
    all_grad = [my_grad, *swap_sequence(my_grad)]
    out_slices = out_slice[None]
    for bit in chip_bits():
        out_slices = jnp.concatenate([out_slices, swap_member(out_slices, bit)], axis=0)
    attended_all = gather_heads(attended_rows, blocks[-1], out_slices)
    out_slices = jnp.concatenate([out_slices, swap_member(out_slices, 1)], axis=0)
    full_out = assemble_out(me_ref, out_slices)

    hidden = inputs + dot(attended_all, full_out, 0, 0)
    normed_two = hidden * inverse_rms(hidden)
    my_xn_two = (normed_two * gain_two).astype(bf16)
    xn_two = [my_xn_two, *swap_sequence(my_xn_two)]

    logits = dot(full_router, my_xn_two, 0, 1)
    named = jnp.any(
        my_routes[:, None, :] == jnp.arange(experts, dtype=jnp.int32)[None, :, None], axis=0
    )
    peak = jnp.max(jnp.where(named, logits, -jnp.inf), axis=0, keepdims=True)
    exps = jnp.where(named, jnp.exp(jnp.minimum(logits - peak, 0.0)), 0.0)
    gates = exps / jnp.sum(exps, axis=0, keepdims=True)
    group = (me & ~1) | low
    my_gates = [
        lax.dynamic_slice_in_dim(v, group * EXP_DEV, EXP_DEV, axis=0)
        for v in (gates, swap_shard(gates))
    ]

    count = 2 * length
    grad_in = None
    gate_grads, expert_grads, scaled = [], [], []
    for js, w in zip(chunks, weights):
        grad_in, s, gg, grads = expert_chunk(
            xn_two, all_grad, my_gates, w, js, grad_in, js is chunks[-1]
        )
        scaled.append(s)
        gate_grads.append(gg)
        expert_grads.append(grads)

    grad_xn_two, halfway = scatter_members(grad_in)
    for i, grads in enumerate(expert_grads):
        if i > 0:
            grads = after(after(grads, expert_grads[i - 1]), halfway)
        expert_grads[i] = scatter_line(grads)
    gate_grads = jnp.tile(jnp.concatenate(gate_grads, axis=0), (members, 1))
    mine = jnp.arange(experts, dtype=jnp.int32)[:, None] // EXP_DEV == group
    gate_grads = jnp.where(mine, gate_grads, 0.0)
    grad_gates = scatter_members(jnp.split(gate_grads, 4, axis=1), axis=1)
    own_gates = gates[:, :rows]
    grad_chosen = own_gates * (grad_gates - jnp.sum(own_gates * grad_gates, axis=0, keepdims=True))
    grad_logits = grad_chosen.astype(bf16)
    grad_xn_two = grad_xn_two + dot(grad_logits, full_router, 0, 1)
    my_hidden = hidden[:rows]

    my_scale = inverse_rms(my_hidden)
    my_normed = my_hidden * my_scale
    grad_gain_two = jnp.sum(grad_xn_two * my_normed, axis=0)
    g = grad_xn_two * gain_two
    grad_hidden = cotangent[0].astype(f32) + my_scale * (
        g - my_normed * jnp.mean(g * my_normed, axis=-1, keepdims=True)
    )
    grad_attn = gather_members(grad_hidden.astype(bf16))
    grad_attended = dot(full_out[:q_cols], grad_attn, 1, 1).astype(bf16)
    grad_attended = grad_attended.reshape(heads, HEAD_SIZE, length)
    grad_out = jnp.dot(attended_rows, grad_attn, preferred_element_type=f32)
    grad_out = jnp.transpose(
        grad_out.astype(bf16).reshape(shards, out_rows, members, q_cols), (0, 2, 1, 3)
    )
    grad_out = split_lines(grad_out.reshape(width, q_cols), low)
    grad_router = dot(my_xn_two[:rows], grad_logits, 0, 1)

    dq, dk, dv = attention_backward(me_ref, queries, keys, values, attended, grad_attended, lse, seg)
    dq = rotate(dq, cosine, -sine) * HEAD_SIZE**-0.5
    dk = rotate(dk, cosine, -sine)
    grad_qkv = jnp.concatenate([dq, dk, dv], axis=0).astype(bf16).reshape(-1, length)
    grad_first = behind = dot(xn_one, grad_qkv, 0, 1)
    grad_xn_one = dot(after(grad_qkv, grad_first), full_qkv, 0, 1)
    grad_gain_one = jnp.sum(grad_xn_one * normed_one, axis=0)
    grad_xn_one = grad_xn_one.astype(bf16)
    for bit in [1] + chip_bits()[::-1]:
        keep, sent = halves(grad_xn_one.astype(bf16), 0)
        grad_xn_one = add_swapped(keep, sent, lambda u: swap_member(u, bit))
    my_inputs = tokens[0].astype(f32)
    scale_one = inverse_rms(my_inputs)
    normed = my_inputs * scale_one
    h = grad_xn_one * gain_one
    grad_tokens = grad_hidden + scale_one * (h - normed * jnp.mean(h * normed, axis=-1, keepdims=True))

    rest = jnp.concatenate([grad_router, grad_gain_one[:, None], grad_gain_two[:, None]], axis=1)
    rest = jnp.pad(rest, ((0, 0), (0, 128 - rest.shape[1])))
    grad_first = jnp.concatenate([grad_first, rest], axis=1).astype(bf16)
    grad_first = jnp.transpose(grad_first.reshape(members, shards, out_rows, -1), (1, 0, 2, 3))
    grad_first = split_lines(grad_first.reshape(width, -1), low)
    grad_first = jnp.concatenate([grad_first, grad_out], axis=1)
    grad_first = scatter_line(after(grad_first, expert_grads[-1])).reshape(members, out_rows, -1)
    out_grads = jnp.transpose(grad_first[:, :, total_cols + 128 :], (1, 0, 2)).astype(f32)
    grad_first = grad_first[:, :, : total_cols + 128]
    grad_first = lax.all_to_all(grad_first, "expert", split_axis=0, concat_axis=0, tiled=True)
    rest = jnp.sum(grad_first[:, :, total_cols:].astype(f32), axis=0)
    grad_first = jnp.transpose(grad_first, (1, 0, 2)).astype(f32)

    mixed = my_hidden + scatter_members(mix_experts(scaled, weights, behind))[0]

    gate_up_out, down_out = [], []
    one = None
    for js, v in zip(chunks, expert_grads):
        if one is not None:
            v, one = lax.optimization_barrier((v, one))
        size = v.shape[0] // 2
        one = permute_all(jnp.where(core == 0, v[:size], v[size:]), turn(True, True))
        two = permute_all(jnp.where(core == 0, v[size:], v[:size]), turn(False, True))
        sides = [jnp.where(low == 0, one, two), jnp.where(low == 0, two, one)]
        n = len(js)
        for i in range(n):
            piece = [
                [sides[h][:, (k * n + i) * half : (k * n + i + 1) * half] for h in range(2)]
                for k in range(3)
            ]
            gate_up_out.append(jnp.concatenate(piece[0] + piece[1], axis=1))
            down_out.append(jnp.concatenate(piece[2], axis=1))
    return (
        mixed.astype(bf16)[None],
        grad_tokens.astype(bf16)[None],
        rest[:, experts],
        grad_first[:, :, :q_cols].reshape(out_rows, -1),
        grad_first[:, :, q_cols : q_cols + k_cols].reshape(out_rows, -1),
        grad_first[:, :, q_cols + k_cols : total_cols].reshape(out_rows, -1),
        out_grads.reshape(out_rows, -1),
        rest[:, experts + 1],
        rest[:, :experts],
        jnp.stack(gate_up_out, axis=1).astype(f32),
        jnp.stack(down_out, axis=1).astype(f32),
    )


def solution(mesh):
    in_specs = (
        P("shard", "expert", None),
        P("shard", "expert"),
        P("shard", "expert", None),
        P("shard"),
        P("shard", None),
        P("shard", None),
        P("shard", None),
        P("shard", None),
        P("shard"),
        P("shard", None),
        P("shard", "expert", None),
        P("shard", "expert", None),
        P("shard", "expert", None),
    )
    out_specs = (
        P("shard", "expert", None),
        P("shard", "expert", None),
        P(("expert", "shard")),
        P(("expert", "shard"), None),
        P(("expert", "shard"), None),
        P(("expert", "shard"), None),
        P(("expert", "shard"), None),
        P(("expert", "shard")),
        P(("expert", "shard"), None),
        P("shard", "expert", None),
        P("shard", "expert", None),
    )
    return jax.shard_map(body, mesh=mesh, in_specs=in_specs, out_specs=out_specs, check_vma=False)
```

```python
import functools

import jax
import jax.numpy as jnp
from jax import lax
from jax.experimental import pallas as pl
from jax.experimental.pallas import tpu as pltpu
from jax.sharding import PartitionSpec as P

QUERY_HEADS = 24
KEY_VALUE_HEADS = 8
GROUP = QUERY_HEADS // KEY_VALUE_HEADS
HEAD_SIZE = 64
HALF = HEAD_SIZE // 2
FF = 512
TOP = 8
EXP_DEV = 5
BLOCK = 256
TILE = 512
BANDS = 4
MASKED = -1e30
epsilon = 1e-06


def dot(a, b, ca, cb):
    return lax.dot_general(a, b, (((ca,), (cb,)), ((), ())), preferred_element_type=jnp.float32)


def inverse_rms(v):
    return lax.rsqrt(jnp.mean(v * v, axis=-1, keepdims=True) + epsilon)


def place_of(block, mine, members):
    r = block ^ mine
    return (r & 1) * (members // 2) + (r >> 1)


def spans(me_ref, blocks):
    return [pl.multiple_of(place_of(a, me_ref[0], blocks) * BLOCK, BLOCK) for a in range(blocks)]


def allowed_tile(seg_col, seg_row, at, qi, ki):
    ok = seg_col[pl.ds(at[ki], BLOCK), :] == seg_row[:, pl.ds(at[qi], BLOCK)]
    if qi == ki:
        kpos = lax.broadcasted_iota(jnp.int32, (BLOCK, BLOCK), 0)
        qpos = lax.broadcasted_iota(jnp.int32, (BLOCK, BLOCK), 1)
        ok = ok & (kpos <= qpos)
    return ok


def attention_forward_kernel(blocks, me_ref, q_ref, k_ref, v_ref, seg_col, seg_row, o_ref, lse_ref, keys):
    at = spans(me_ref, blocks)
    keys[...] = k_ref[0].astype(jnp.float32).T.astype(jnp.bfloat16)
    for qi in range(blocks):
        qs = pl.ds(at[qi], BLOCK)
        q = q_ref[0, :, qs]
        top = total = acc = None
        for ki in range(qi, -1, -1):
            ks = pl.ds(at[ki], BLOCK)
            s = dot(keys[ks, :], q, 1, 0)
            s = jnp.where(allowed_tile(seg_col, seg_row, at, qi, ki), s, MASKED)
            peak = jnp.max(s, axis=0, keepdims=True)
            if top is None:
                top = peak
                e = jnp.exp(s - top)
                total = jnp.sum(e, axis=0, keepdims=True)
                acc = dot(v_ref[0, :, ks], e.astype(jnp.bfloat16), 1, 0)
            else:
                new = jnp.maximum(top, peak)
                scale = jnp.exp(top - new)
                e = jnp.exp(s - new)
                total = total * scale + jnp.sum(e, axis=0, keepdims=True)
                acc = acc * scale + dot(v_ref[0, :, ks], e.astype(jnp.bfloat16), 1, 0)
                top = new
        o_ref[0, :, qs] = (acc / total).astype(jnp.bfloat16)
        lse_ref[0, :, qs] = top + jnp.log(total)


def attention_forward(me, q, k, v, seg):
    heads, _, length = q.shape
    blocks = length // BLOCK
    full = pl.BlockSpec((1, HEAD_SIZE, length), lambda h, me: (h, 0, 0))
    shared = pl.BlockSpec((1, HEAD_SIZE, length), lambda h, me: (h // GROUP, 0, 0))
    return pl.pallas_call(
        functools.partial(attention_forward_kernel, blocks),
        grid_spec=pltpu.PrefetchScalarGridSpec(
            num_scalar_prefetch=1,
            grid=(heads,),
            in_specs=[
                full,
                shared,
                shared,
                pl.BlockSpec((length, 1), lambda h, me: (0, 0)),
                pl.BlockSpec((1, length), lambda h, me: (0, 0)),
            ],
            out_specs=[full, pl.BlockSpec((1, 1, length), lambda h, me: (h, 0, 0))],
            scratch_shapes=[pltpu.VMEM((length, HEAD_SIZE), jnp.bfloat16)],
        ),
        out_shape=[
            jax.ShapeDtypeStruct((heads, HEAD_SIZE, length), jnp.bfloat16),
            jax.ShapeDtypeStruct((heads, 1, length), jnp.float32),
        ],
        compiler_params=pltpu.CompilerParams(vmem_limit_bytes=48 * 1024 * 1024),
        cost_estimate=pl.CostEstimate(
            flops=50 * heads * length * length * HEAD_SIZE,
            bytes_accessed=6 * heads * length * HEAD_SIZE,
            transcendentals=heads * length * length // 2,
        ),
        name="attention_forward",
    )(me, q, k, v, seg[:, None], seg[None, :])


def attention_backward_kernel(
    blocks, me_ref, q_ref, k_ref, v_ref, o_ref, g_ref, lse_ref, seg_col, seg_row,
    dq_ref, dk_ref, dv_ref, keys, values, dk_acc, dv_acc,
):
    at = spans(me_ref, blocks)
    member = pl.program_id(1)

    @pl.when(member == 0)
    def _():
        dk_acc[...] = jnp.zeros_like(dk_acc)
        dv_acc[...] = jnp.zeros_like(dv_acc)
        keys[...] = k_ref[0].astype(jnp.float32).T.astype(jnp.bfloat16)
        values[...] = v_ref[0].astype(jnp.float32).T.astype(jnp.bfloat16)

    for qi in range(blocks):
        qs = pl.ds(at[qi], BLOCK)
        q = q_ref[0, :, qs]
        g = g_ref[0, :, qs]
        g32 = g.astype(jnp.float32)
        delta = jnp.sum(g32 * o_ref[0, :, qs].astype(jnp.float32), axis=0, keepdims=True)
        lse = lse_ref[0, :, qs]
        q_rows = q.astype(jnp.float32).T.astype(jnp.bfloat16)
        g_rows = g32.T.astype(jnp.bfloat16)
        dq = jnp.zeros((HEAD_SIZE, BLOCK), jnp.float32)
        for ki in range(qi + 1):
            ks = pl.ds(at[ki], BLOCK)
            s = dot(keys[ks, :], q, 1, 0)
            p = jnp.where(allowed_tile(seg_col, seg_row, at, qi, ki), jnp.exp(s - lse), 0.0)
            dp = dot(values[ks, :], g, 1, 0)
            ds = (p * (dp - delta)).astype(jnp.bfloat16)
            dv_acc[ks, :] += dot(p.astype(jnp.bfloat16), g_rows, 1, 0)
            dk_acc[ks, :] += dot(ds, q_rows, 1, 0)
            dq = dq + dot(k_ref[0, :, ks], ds, 1, 0)
        dq_ref[0, :, qs] = dq

    @pl.when(member == GROUP - 1)
    def _():
        dk_ref[0] = dk_acc[...].T
        dv_ref[0] = dv_acc[...].T


def attention_backward(me, q, k, v, o, g, lse, seg):
    heads, _, length = q.shape
    blocks = length // BLOCK
    full = pl.BlockSpec((1, HEAD_SIZE, length), lambda j, m, me: (j * GROUP + m, 0, 0))
    shared = pl.BlockSpec((1, HEAD_SIZE, length), lambda j, m, me: (j, 0, 0))
    return pl.pallas_call(
        functools.partial(attention_backward_kernel, blocks),
        grid_spec=pltpu.PrefetchScalarGridSpec(
            num_scalar_prefetch=1,
            grid=(heads // GROUP, GROUP),
            in_specs=[
                full,
                shared,
                shared,
                full,
                full,
                pl.BlockSpec((1, 1, length), lambda j, m, me: (j * GROUP + m, 0, 0)),
                pl.BlockSpec((length, 1), lambda j, m, me: (0, 0)),
                pl.BlockSpec((1, length), lambda j, m, me: (0, 0)),
            ],
            out_specs=[full, shared, shared],
            scratch_shapes=[
                pltpu.VMEM((length, HEAD_SIZE), jnp.bfloat16),
                pltpu.VMEM((length, HEAD_SIZE), jnp.bfloat16),
                pltpu.VMEM((length, HEAD_SIZE), jnp.float32),
                pltpu.VMEM((length, HEAD_SIZE), jnp.float32),
            ],
        ),
        out_shape=[
            jax.ShapeDtypeStruct((heads, HEAD_SIZE, length), jnp.float32),
            jax.ShapeDtypeStruct((heads // GROUP, HEAD_SIZE, length), jnp.float32),
            jax.ShapeDtypeStruct((heads // GROUP, HEAD_SIZE, length), jnp.float32),
        ],
        compiler_params=pltpu.CompilerParams(vmem_limit_bytes=48 * 1024 * 1024),
        cost_estimate=pl.CostEstimate(
            flops=46 * heads * length * length * HEAD_SIZE,
            bytes_accessed=16 * heads * length * HEAD_SIZE,
            transcendentals=heads * length * length // 2,
        ),
        name="attention_backward",
    )(me, q, k, v, o, g, lse, seg[:, None], seg[None, :])


def rope_tables(positions):
    freqs = 10000.0 ** (-(jnp.arange(HALF, dtype=jnp.float32) * 2.0 / HEAD_SIZE))
    angles = freqs[:, None] * positions.astype(jnp.float32)[None, :]
    return jnp.cos(angles)[None], jnp.sin(angles)[None]


def rotate(v, cosine, sine):
    a, b = v[:, :HALF, :], v[:, HALF:, :]
    return jnp.concatenate([a * cosine - b * sine, b * cosine + a * sine], axis=1)


def side_tiles(tiles):
    return [(0, tiles // 2), (tiles // 2, tiles // 4), (3 * tiles // 4, tiles // 4)]


def expert_kernel(start, n, half, tiles, band, has_in, parts, *refs):
    refs = list(refs)
    x_refs = refs[:3]
    g_refs = refs[3:6]
    wt_refs = refs[6:8]
    w_ref = refs[8]
    refs = refs[9:]
    gin_in = refs.pop(0) if has_in else None
    gin_refs, refs = refs[:parts], refs[parts:]
    s_ref, gg_ref, dw_ref, xs, gs, ss, bs, sems = refs
    step = pl.program_id(0)
    later = step - tiles
    m = 2 * n * half
    arrivals = []
    for side, (first, size) in enumerate(side_tiles(tiles)):
        for i in range(size):
            to = slice((first + i) * TILE, (first + i + 1) * TILE)
            arrivals.append(
                [
                    pltpu.make_async_copy(
                        sources[side].at[slice(i * TILE, (i + 1) * TILE), :],
                        target.at[to, :],
                        sems.at[k, first + i],
                    )
                    for k, (sources, target) in enumerate(((x_refs, xs), (g_refs, gs)))
                ]
            )

    @pl.when(step == 0)
    def _():
        for pair in arrivals:
            for copy in pair:
                copy.start()

    for i, pair in enumerate(arrivals):

        @pl.when(step == i)
        def _():
            for copy in pair:
                copy.wait()

    @pl.when(step < tiles)
    def _():
        at = pl.ds(pl.multiple_of(step * TILE, TILE), TILE)
        x = xs[at, :]
        g = gs[at, :]
        weights = jnp.where(step < tiles // 2, wt_refs[0][...], wt_refs[1][...]).T
        sums = []
        for i in range(n):
            c = [slice((k * n + i) * half, (k * n + i + 1) * half) for k in range(3)]
            gate = dot(x, w_ref[:, c[0]], 1, 0)
            up = dot(x, w_ref[:, c[1]], 1, 0)
            through = dot(g, w_ref[:, c[2]], 1, 0)
            weight = weights[:, start + i : start + i + 1]
            sig = jax.nn.sigmoid(gate)
            soft = gate * sig
            act = soft * up
            sums.append(jnp.sum(act * through, axis=1, keepdims=True))
            scaled = (weight * act).astype(jnp.bfloat16)
            ss[at, c[0]] = scaled
            s_ref[:, c[0]] = scaled
            grad = weight * through
            bs[at, c[0]] = (grad * up * sig * (1.0 + gate * (1.0 - sig))).astype(jnp.bfloat16)
            bs[at, c[1]] = (grad * soft).astype(jnp.bfloat16)
        gg_ref[...] = jnp.concatenate(sums, axis=1).T

    @pl.when(later >= 0)
    def _():
        tile = tiles - 1 - later
        at = pl.ds(pl.multiple_of(tile * TILE, TILE), TILE)
        gin = dot(bs[at, :], w_ref[:, :m], 1, 1)
        if has_in:
            gin = gin + gin_in[...]
        if parts == 1:
            gin_refs[0][...] = gin
        else:
            for part in range(parts):

                @pl.when(tile * parts // tiles == part)
                def _():
                    gin_refs[part][...] = gin.astype(jnp.bfloat16)

    @pl.when((later >= 0) & (later < BANDS))
    def _():
        at = pl.ds(pl.multiple_of(later * band, band), band)
        dw_ref[:, :m] = dot(xs[:, at], bs[...], 0, 0).astype(jnp.bfloat16)
        dw_ref[:, m:] = dot(gs[:, at], ss[...], 0, 0).astype(jnp.bfloat16)


def expert_chunk(xs, gs, wts, w, js, carried, last):
    length, width = xs[0].shape
    count = 2 * length
    n = len(js)
    half = w.shape[1] // (3 * n)
    tiles = count // TILE
    band = width // BANDS
    parts = 4 if last else 1
    sub = tiles // parts

    def early(size):
        return pl.BlockSpec((TILE, size), lambda i: (jnp.minimum(i, tiles - 1), 0))

    weight_sides = [
        pl.BlockSpec((EXP_DEV, TILE), lambda i, f=first: (0, jnp.clip(i - f, 0, tiles // 2 - 1)))
        for first in (0, tiles // 2)
    ]

    def late(part):
        return pl.BlockSpec(
            (TILE, width),
            lambda i: (jnp.clip(tiles - 1 - jnp.maximum(i - tiles, 0) - part * sub, 0, tiles // parts - 1), 0),
        )

    args = [*xs, *gs, *wts, w]
    specs = [
        *[pl.BlockSpec(memory_space=pl.ANY)] * 6,
        *weight_sides,
        pl.BlockSpec(w.shape, lambda i: (0, 0), pipeline_mode=pl.Buffered(1)),
    ]
    if carried is not None:
        args.append(carried)
        specs.append(
            pl.BlockSpec((TILE, width), lambda i: (tiles - 1 - jnp.maximum(i - tiles, 0), 0))
        )
    out = pl.pallas_call(
        functools.partial(expert_kernel, js[0], n, half, tiles, band, carried is not None, parts),
        grid=(2 * tiles,),
        in_specs=specs,
        out_specs=[
            *[late(part) for part in range(parts)],
            early(n * half),
            pl.BlockSpec((n, TILE), lambda i: (0, jnp.minimum(i, tiles - 1))),
            pl.BlockSpec((band, w.shape[1]), lambda i: (jnp.clip(i - tiles, 0, BANDS - 1), 0)),
        ],
        out_shape=[
            *[
                jax.ShapeDtypeStruct((count // parts, width), jnp.bfloat16 if last else jnp.float32)
                for _ in range(parts)
            ],
            jax.ShapeDtypeStruct((count, n * half), jnp.bfloat16),
            jax.ShapeDtypeStruct((n, count), jnp.float32),
            jax.ShapeDtypeStruct(w.shape, jnp.bfloat16),
        ],
        scratch_shapes=[
            pltpu.VMEM((count, width), jnp.bfloat16),
            pltpu.VMEM((count, width), jnp.bfloat16),
            pltpu.VMEM((count, n * half), jnp.bfloat16),
            pltpu.VMEM((count, 2 * n * half), jnp.bfloat16),
            pltpu.SemaphoreType.DMA((2, tiles)),
        ],
        compiler_params=pltpu.CompilerParams(vmem_limit_bytes=60 * 1024 * 1024),
        cost_estimate=pl.CostEstimate(
            flops=16 * count * n * half * width,
            bytes_accessed=8 * count * width + 4 * width * n * half * 3,
            transcendentals=count * n * half,
        ),
        name="experts",
    )(*args)
    return (out[:parts] if last else out[0]), *out[parts:]


def mix_kernel(n, parts, *refs):
    refs = refs[: 2 * n] + refs[2 * n + 1 :]
    total = dot(refs[0][...], refs[n][...], 1, 1)
    for i in range(1, n):
        total = total + dot(refs[i][...], refs[n + i][...], 1, 1)
    step, steps = pl.program_id(0), pl.num_programs(0)
    for part in range(parts):

        @pl.when((steps - 1 - step) * parts // steps == part)
        def _():
            refs[2 * n + part][...] = total.astype(jnp.bfloat16)


def mix_experts(scaled, weights, behind):
    count, width = scaled[0].shape[0], weights[0].shape[0]
    n, parts, steps = len(scaled), 4, count // TILE
    sub = steps // parts

    def late(part):
        return pl.BlockSpec((TILE, width), lambda i: (jnp.clip(steps - 1 - i - part * sub, 0, sub - 1), 0))

    return pl.pallas_call(
        functools.partial(mix_kernel, n, parts),
        grid=(steps,),
        in_specs=[pl.BlockSpec((TILE, s.shape[1]), lambda i: (steps - 1 - i, 0)) for s in scaled]
        + [pl.BlockSpec((width, s.shape[1]), lambda i: (0, 2)) for s in scaled]
        + [pl.BlockSpec(memory_space=pl.ANY)],
        out_specs=[late(part) for part in range(parts)],
        out_shape=[jax.ShapeDtypeStruct((count // parts, width), jnp.bfloat16) for _ in range(parts)],
        compiler_params=pltpu.CompilerParams(vmem_limit_bytes=60 * 1024 * 1024),
        cost_estimate=pl.CostEstimate(
            flops=4 * count * width * sum(s.shape[1] for s in scaled),
            bytes_accessed=4 * count * width,
            transcendentals=0,
        ),
        name="mix_experts",
    )(*scaled, *weights, behind)


def swap_member(v, bit):
    n = lax.axis_size("expert")
    return lax.ppermute(v, "expert", [(i, i ^ bit) for i in range(n)])


def swap_shard(v):
    n = lax.axis_size("shard")
    return lax.ppermute(v, "shard", [(i, i ^ 1) for i in range(n)])


def after(v, behind):
    return pl.pallas_call(
        lambda *refs: None,
        in_specs=[pl.BlockSpec(memory_space=pl.ANY)] * 2,
        out_specs=pl.BlockSpec(memory_space=pl.ANY),
        out_shape=jax.ShapeDtypeStruct(v.shape, v.dtype),
        input_output_aliases={0: 0},
        cost_estimate=pl.CostEstimate(flops=0, bytes_accessed=1024, transcendentals=0),
        name="after",
    )(v, behind)


def swap_sequence(v):
    got = swap_shard(v[: v.shape[0] // 2])
    return [got, swap_member(got, 1)]


def chip_bits():
    n = lax.axis_size("expert")
    return [1 << i for i in range(1, n.bit_length() - 1)]


def gather_members(v, axis=0):
    for bit in chip_bits() + [1]:
        v = jnp.concatenate([v, swap_member(v, bit)], axis=axis)
    return v


def gather_heads(v, *behind):
    members = lax.axis_size("expert")
    width = v.shape[1] // members
    for bit in chip_bits() + [1]:
        if bit == 1:
            for other in behind:
                v = after(v, other)
        got = swap_member(v, bit)
        source = [place_of(2 * (p % (members // 2)) + p // (members // 2), bit, members) for p in range(members)]
        got = jnp.concatenate([got[:, p * width : (p + 1) * width] for p in source], axis=1)
        v = jnp.concatenate([v, got], axis=0)
    return v


def halves(v, axis):
    return jnp.split(v, 2, axis=axis)


def add_swapped(keep, sent, swap):
    return keep.astype(jnp.float32) + swap(sent).astype(jnp.float32)


def scatter_chip(v, axis):
    for bit in reversed(chip_bits()):
        keep, sent = halves(v, axis)
        v = add_swapped(keep, sent, lambda u: swap_member(u, bit)).astype(v.dtype)
    return v


def scatter_members(parts, axis=0):
    kind = parts[0].dtype
    other = add_swapped(parts[2], parts[3], lambda u: swap_member(u, 1)).astype(kind)
    own = add_swapped(parts[0], parts[1], lambda u: swap_member(u, 1)).astype(kind)
    if axis == 1:
        return scatter_chip(add_swapped(own, other, swap_shard), axis)
    cut = own.shape[1] // 2
    one = add_swapped(own[:, :cut], other[:, :cut], swap_shard).astype(kind)
    halfway = one
    one = scatter_chip(one, 0)
    two, two_other = scatter_chip(own[:, cut:], 0), scatter_chip(other[:, cut:], 0)
    two = add_swapped(two, two_other, swap_shard)
    return jnp.concatenate([one.astype(jnp.float32), two], axis=1), halfway


def turn(first, back=False):
    members, shards = lax.axis_size("expert"), lax.axis_size("shard")
    pairs = []
    for e in range(members):
        for s in range(shards):
            core, low = e & 1, s & 1
            to_core, to_low = (low, core) if first else (1 - low, core)
            target = ((e & ~1) | to_core) * shards + ((s & ~1) | to_low)
            pairs.append((e * shards + s, target))
    if back:
        pairs = [(b, a) for a, b in pairs]
    return pairs


def permute_all(v, pairs):
    return lax.ppermute(v, ("expert", "shard"), pairs)


def shard_lines():
    n = lax.axis_size("shard")
    return [[s for s in range(n) if s & 1 == low] for low in range(2)]


def gather_line(v):
    return lax.all_gather(v, "shard", axis=0, tiled=True, axis_index_groups=shard_lines())


def scatter_line(v):
    return lax.psum_scatter(
        v, "shard", scatter_dimension=0, tiled=True, axis_index_groups=shard_lines()
    )


def merge_lines(v, low):
    n = lax.axis_size("shard") // 2
    got = swap_shard(v)
    v, got = v.reshape(n, -1, v.shape[1]), got.reshape(n, -1, v.shape[1])
    sides = [jnp.where(low == 0, v, got), jnp.where(low == 0, got, v)]
    return jnp.stack(sides, axis=1).reshape(-1, v.shape[2])


def split_lines(v, low):
    n = lax.axis_size("shard") // 2
    v = v.reshape(n, 2, -1, v.shape[1])
    keep, sent = jnp.where(low == 0, v[:, 0], v[:, 1]), jnp.where(low == 0, v[:, 1], v[:, 0])
    keep, sent = keep.reshape(-1, v.shape[3]), sent.reshape(-1, v.shape[3])
    return add_swapped(keep, sent, swap_shard).astype(v.dtype)


def out_kernel(members, me_ref, slice_ref, out_ref):
    size = slice_ref.shape[2]
    p = pl.program_id(0)
    r = 2 * (p % (members // 2)) + p // (members // 2)
    col = pl.multiple_of((me_ref[0] ^ r) * size, 128)
    for a in range(members):
        row = pl.multiple_of(place_of(a, me_ref[0], members) * size, 16)
        out_ref[pl.ds(row, size), pl.ds(col, size)] = slice_ref[0, a * size : (a + 1) * size, :]


def assemble_out(me, slices):
    members, rows, size = slices.shape
    return pl.pallas_call(
        functools.partial(out_kernel, members),
        grid_spec=pltpu.PrefetchScalarGridSpec(
            num_scalar_prefetch=1,
            grid=(members,),
            in_specs=[pl.BlockSpec((1, rows, size), lambda p, me: (p, 0, 0))],
            out_specs=pl.BlockSpec((rows, size * members), lambda p, me: (0, 0)),
        ),
        out_shape=jax.ShapeDtypeStruct((rows, size * members), slices.dtype),
        compiler_params=pltpu.CompilerParams(vmem_limit_bytes=48 * 1024 * 1024),
        cost_estimate=pl.CostEstimate(
            flops=0, bytes_accessed=4 * rows * size * members, transcendentals=0
        ),
        name="assemble_out",
    )(me, slices)


def body(
    tokens,
    segment_ids,
    routes,
    gain_attn,
    w_query,
    key_weight,
    value_weight,
    w_out,
    gain_ffn,
    w_router,
    w_gate_up,
    w_down,
    cotangent,
):
    bf16, f32 = jnp.bfloat16, jnp.float32
    members = lax.axis_size("expert")
    shards = lax.axis_size("shard")
    me = lax.axis_index("expert")
    core = me & 1
    low = lax.axis_index("shard") & 1
    rows, width = tokens.shape[1:]
    length = rows * members
    experts = EXP_DEV * members
    q_cols = QUERY_HEADS * HEAD_SIZE // members
    k_cols = KEY_VALUE_HEADS * HEAD_SIZE // members
    heads, kv_heads = q_cols // HEAD_SIZE, k_cols // HEAD_SIZE
    out_rows = width // (members * shards)
    half = FF // 2
    cuts = [0, 2, EXP_DEV] if length <= 1024 else range(EXP_DEV + 1)
    chunks = [tuple(range(a, b)) for a, b in zip(cuts[:-1], cuts[1:])]
    me_ref = me[None].astype(jnp.int32)

    def cols(w, n):
        return lax.dynamic_slice_in_dim(w, me * n, n, axis=1)

    all_tokens = gather_members(tokens[0])
    meta = jnp.concatenate([segment_ids, routes[0].T], axis=0)
    meta = gather_members(meta, axis=1)
    seg = meta[0]
    my_routes = meta[1:]
    my_grad = after(cotangent[0], all_tokens)
    for bit in chip_bits():
        my_grad = jnp.concatenate([my_grad, swap_member(my_grad, bit)], axis=0)
    grad_pair = my_grad
    my_grad = jnp.concatenate([my_grad, swap_member(my_grad, 1)], axis=0)

    small = jnp.concatenate([w_router, gain_attn[:, None], gain_ffn[:, None]], axis=1)
    total_cols = q_cols + 2 * k_cols
    first = jnp.concatenate(
        [
            cols(w_out, q_cols),
            cols(w_query, q_cols),
            cols(key_weight, k_cols),
            cols(value_weight, k_cols),
            jnp.pad(small, ((0, 0), (0, 128 - small.shape[1]))),
        ],
        axis=1,
    )
    first = gather_line(first)
    out_slice = first[:, :q_cols]
    first = merge_lines(after(first[:, q_cols:], grad_pair), low)
    out_slice = merge_lines(after(out_slice, first), low)
    full_qkv = first[:, :total_cols]
    full_small = first[:, total_cols:]
    full_router = full_small[:, :experts]
    gain_one = full_small[:, experts].astype(f32)
    gain_two = full_small[:, experts + 1].astype(f32)

    weights, blocks = [], []
    for js in chunks:
        sides = [
            jnp.concatenate(
                [w_gate_up[:, j, h * half : (h + 1) * half] for j in js]
                + [w_gate_up[:, j, FF + h * half : FF + (h + 1) * half] for j in js]
                + [w_down[:, j, h * half : (h + 1) * half] for j in js],
                axis=1,
            )
            for h in range(2)
        ]
        one = jnp.where(low == 0, sides[0], sides[1])
        two = jnp.where(low == 0, sides[1], sides[0])
        if blocks:
            one, two = after(one, out_slice), after(two, out_slice)
        one, two = permute_all(one, turn(True)), permute_all(two, turn(False))
        block = jnp.concatenate(
            [jnp.where(core == 0, one, two), jnp.where(core == 0, two, one)], axis=0
        )
        blocks.append(block)
        weights.append(
            gather_line(block)
        )

    inputs = all_tokens.astype(f32)
    normed_one = inputs * inverse_rms(inputs)
    xn_one = (normed_one * gain_one).astype(bf16)
    qkv = dot(full_qkv, xn_one, 0, 1).reshape(heads + 2 * kv_heads, HEAD_SIZE, length)
    order = jnp.arange(members, dtype=jnp.int32)
    order = me ^ (2 * (order % (members // 2)) + order // (members // 2))
    positions = (order[:, None] * rows + jnp.arange(rows, dtype=jnp.int32)[None, :]).reshape(-1)
    cosine, sine = rope_tables(positions)
    rotated = rotate(qkv[: heads + kv_heads], cosine, sine).astype(bf16)
    queries = rotated[:heads] * jnp.asarray(HEAD_SIZE**-0.5, bf16)
    keys = rotated[heads:]
    values = qkv[heads + kv_heads :].astype(bf16)
    attended, lse = attention_forward(me_ref, queries, keys, values, seg)
    attended_rows = attended.reshape(q_cols, length)
    all_grad = [my_grad, *swap_sequence(my_grad)]
    out_slices = out_slice[None]
    for bit in chip_bits():
        out_slices = jnp.concatenate([out_slices, swap_member(out_slices, bit)], axis=0)
    attended_all = gather_heads(attended_rows, blocks[-1], out_slices)
    out_slices = jnp.concatenate([out_slices, swap_member(out_slices, 1)], axis=0)
    full_out = assemble_out(me_ref, out_slices)

    hidden = inputs + dot(attended_all, full_out, 0, 0)
    normed_two = hidden * inverse_rms(hidden)
    my_xn_two = (normed_two * gain_two).astype(bf16)
    xn_two = [my_xn_two, *swap_sequence(my_xn_two)]

    logits = dot(full_router, my_xn_two, 0, 1)
    named = jnp.any(
        my_routes[:, None, :] == jnp.arange(experts, dtype=jnp.int32)[None, :, None], axis=0
    )
    peak = jnp.max(jnp.where(named, logits, -jnp.inf), axis=0, keepdims=True)
    exps = jnp.where(named, jnp.exp(jnp.minimum(logits - peak, 0.0)), 0.0)
    gates = exps / jnp.sum(exps, axis=0, keepdims=True)
    group = (me & ~1) | low
    my_gates = [
        lax.dynamic_slice_in_dim(v, group * EXP_DEV, EXP_DEV, axis=0)
        for v in (gates, swap_shard(gates))
    ]

    count = 2 * length
    grad_in = None
    gate_grads, expert_grads, scaled = [], [], []
    for js, w in zip(chunks, weights):
        grad_in, s, gg, grads = expert_chunk(
            xn_two, all_grad, my_gates, w, js, grad_in, js is chunks[-1]
        )
        scaled.append(s)
        gate_grads.append(gg)
        expert_grads.append(grads)

    grad_xn_two, halfway = scatter_members(grad_in)
    for i, grads in enumerate(expert_grads):
        if i > 0:
            grads = after(after(grads, expert_grads[i - 1]), halfway)
        expert_grads[i] = scatter_line(grads)
    gate_grads = jnp.tile(jnp.concatenate(gate_grads, axis=0), (members, 1))
    mine = jnp.arange(experts, dtype=jnp.int32)[:, None] // EXP_DEV == group
    gate_grads = jnp.where(mine, gate_grads, 0.0)
    grad_gates = scatter_members(jnp.split(gate_grads, 4, axis=1), axis=1)
    own_gates = gates[:, :rows]
    grad_chosen = own_gates * (grad_gates - jnp.sum(own_gates * grad_gates, axis=0, keepdims=True))
    grad_logits = grad_chosen.astype(bf16)
    grad_xn_two = grad_xn_two + dot(grad_logits, full_router, 0, 1)
    my_hidden = hidden[:rows]

    my_scale = inverse_rms(my_hidden)
    my_normed = my_hidden * my_scale
    grad_gain_two = jnp.sum(grad_xn_two * my_normed, axis=0)
    g = grad_xn_two * gain_two
    grad_hidden = cotangent[0].astype(f32) + my_scale * (
        g - my_normed * jnp.mean(g * my_normed, axis=-1, keepdims=True)
    )
    grad_attn = gather_members(grad_hidden.astype(bf16))
    grad_attended = dot(full_out[:q_cols], grad_attn, 1, 1).astype(bf16)
    grad_attended = grad_attended.reshape(heads, HEAD_SIZE, length)
    grad_out = jnp.dot(attended_rows, grad_attn, preferred_element_type=f32)
    grad_out = jnp.transpose(
        grad_out.astype(bf16).reshape(shards, out_rows, members, q_cols), (0, 2, 1, 3)
    )
    grad_out = split_lines(grad_out.reshape(width, q_cols), low)
    grad_router = dot(my_xn_two[:rows], grad_logits, 0, 1)

    dq, dk, dv = attention_backward(me_ref, queries, keys, values, attended, grad_attended, lse, seg)
    dq = rotate(dq, cosine, -sine) * HEAD_SIZE**-0.5
    dk = rotate(dk, cosine, -sine)
    grad_qkv = jnp.concatenate([dq, dk, dv], axis=0).astype(bf16).reshape(-1, length)
    grad_first = behind = dot(xn_one, grad_qkv, 0, 1)
    grad_xn_one = dot(after(grad_qkv, grad_first), full_qkv, 0, 1)
    grad_gain_one = jnp.sum(grad_xn_one * normed_one, axis=0)
    grad_xn_one = grad_xn_one.astype(bf16)
    for bit in [1] + chip_bits()[::-1]:
        keep, sent = halves(grad_xn_one.astype(bf16), 0)
        grad_xn_one = add_swapped(keep, sent, lambda u: swap_member(u, bit))
    my_inputs = tokens[0].astype(f32)
    scale_one = inverse_rms(my_inputs)
    normed = my_inputs * scale_one
    h = grad_xn_one * gain_one
    grad_tokens = grad_hidden + scale_one * (h - normed * jnp.mean(h * normed, axis=-1, keepdims=True))

    rest = jnp.concatenate([grad_router, grad_gain_one[:, None], grad_gain_two[:, None]], axis=1)
    rest = jnp.pad(rest, ((0, 0), (0, 128 - rest.shape[1])))
    grad_first = jnp.concatenate([grad_first, rest], axis=1).astype(bf16)
    grad_first = jnp.transpose(grad_first.reshape(members, shards, out_rows, -1), (1, 0, 2, 3))
    grad_first = split_lines(grad_first.reshape(width, -1), low)
    grad_first = jnp.concatenate([grad_first, grad_out], axis=1)
    grad_first = scatter_line(after(grad_first, expert_grads[-1])).reshape(members, out_rows, -1)
    out_grads = jnp.transpose(grad_first[:, :, total_cols + 128 :], (1, 0, 2)).astype(f32)
    grad_first = grad_first[:, :, : total_cols + 128]
    grad_first = lax.all_to_all(grad_first, "expert", split_axis=0, concat_axis=0, tiled=True)
    rest = jnp.sum(grad_first[:, :, total_cols:].astype(f32), axis=0)
    grad_first = jnp.transpose(grad_first, (1, 0, 2)).astype(f32)

    mixed = my_hidden + scatter_members(mix_experts(scaled, weights, behind))[0]

    gate_up_out, down_out = [], []
    one = None
    for js, v in zip(chunks, expert_grads):
        if one is not None:
            v, one = lax.optimization_barrier((v, one))
        size = v.shape[0] // 2
        one = permute_all(jnp.where(core == 0, v[:size], v[size:]), turn(True, True))
        two = permute_all(jnp.where(core == 0, v[size:], v[:size]), turn(False, True))
        sides = [jnp.where(low == 0, one, two), jnp.where(low == 0, two, one)]
        n = len(js)
        for i in range(n):
            piece = [
                [sides[h][:, (k * n + i) * half : (k * n + i + 1) * half] for h in range(2)]
                for k in range(3)
            ]
            gate_up_out.append(jnp.concatenate(piece[0] + piece[1], axis=1))
            down_out.append(jnp.concatenate(piece[2], axis=1))
    return (
        mixed.astype(bf16)[None],
        grad_tokens.astype(bf16)[None],
        rest[:, experts],
        grad_first[:, :, :q_cols].reshape(out_rows, -1),
        grad_first[:, :, q_cols : q_cols + k_cols].reshape(out_rows, -1),
        grad_first[:, :, q_cols + k_cols : total_cols].reshape(out_rows, -1),
        out_grads.reshape(out_rows, -1),
        rest[:, experts + 1],
        rest[:, :experts],
        jnp.stack(gate_up_out, axis=1).astype(f32),
        jnp.stack(down_out, axis=1).astype(f32),
    )


def solution(mesh):
    in_specs = (
        P("shard", "expert", None),
        P("shard", "expert"),
        P("shard", "expert", None),
        P("shard"),
        P("shard", None),
        P("shard", None),
        P("shard", None),
        P("shard", None),
        P("shard"),
        P("shard", None),
        P("shard", "expert", None),
        P("shard", "expert", None),
        P("shard", "expert", None),
    )
    out_specs = (
        P("shard", "expert", None),
        P("shard", "expert", None),
        P(("expert", "shard")),
        P(("expert", "shard"), None),
        P(("expert", "shard"), None),
        P(("expert", "shard"), None),
        P(("expert", "shard"), None),
        P(("expert", "shard")),
        P(("expert", "shard"), None),
        P("shard", "expert", None),
        P("shard", "expert", None),
    )
    return jax.shard_map(body, mesh=mesh, in_specs=in_specs, out_specs=out_specs, check_vma=False)
```
